32 devices in a mesh: section: 8 (over z, y), dp: 4 (over x, core).
Axes of the slice: x: 2, y: 2, z: 4, core: 2. Of those that a mesh axis runs over, the one named last changes fastest.
Arguments:
- saved_input: bfloat16 [8, 512, 12288], P('section', 'dp'), may hold values from -6 to 6
- norm_gain: float32 [8, 12288], P('section'), may hold values from 0.25 to 1.75
- left_in: bfloat16 [8, 512, 64], P('section', 'dp'), may hold values from -6 to 6
- right_in: bfloat16 [8, 12288, 64], P('section', 'dp'), may hold values from -0.75 to 0.75
- basis: bfloat16 [8, 12288, 64], P('section', 'dp'), may hold values from -0.0546875 to 0.0546875
Outputs:
- gain_grad: float32 [8, 12288], P('section', 'dp')
- bias_grad: float32 [8, 12288], P('section', 'dp')
- left_out: bfloat16 [8, 512, 64], P('section', 'dp')
- right_out: bfloat16 [8, 12288, 64], P('section', 'dp')
The draws below stay inside these ranges and needn't reach their ends.
All inputs are finite; a program needn't handle non-finite values.
Results may differ from the reference program's by a relative error of at most 0.02.
Values may be sent and summed in bfloat16 or wider, within the bound.
A program may use at most 64 MiB of HBM per device.

```python
import jax
import jax.numpy as jnp
from jax import lax

D = 12288
R = 64
TOKENS = 512
SECTIONS = 8


def shard_levels(own_key, dims, shards, least, top_value):
    def one(position, shards_of):
        steps = jax.random.uniform(jax.random.fold_in(jax.random.fold_in(own_key, 6), position), (shards_of,), jnp.float32, least / len(shards), top_value / len(shards))
        return jnp.repeat(jnp.exp(steps), dims[position] // shards_of).reshape((-1,) + (1,) * (len(dims) - position - 1))

    level = one(*shards[0])
    for cut in shards[1:]:
        level = level * one(*cut)
    return level


def normal_values(own_key, extent, width, bound, cuts=(), kind=jnp.bfloat16):
    array = width * jax.random.normal(own_key, extent, jnp.float32)
    if cuts:
        array = array * shard_levels(own_key, extent, cuts, -0.22, 0.18)
    return jnp.clip(array, -bound, bound).astype(kind)


def setup_inputs(seed: int = 0) -> dict:
    arg_keys = jax.random.split(jax.random.key(seed), 6)
    saved_input = normal_values(arg_keys[0], (SECTIONS, TOKENS, D), 1.0, 6.0, ((0, 8), (1, 4)))
    norm_gain = jnp.clip(1.0 + 0.15 * jax.random.normal(arg_keys[1], (SECTIONS, D), jnp.float32), 0.25, 1.75)
    left_in = normal_values(arg_keys[2], (SECTIONS, TOKENS, R), 1.0, 6.0, ((0, 8), (1, 4)))
    right_in = normal_values(arg_keys[3], (SECTIONS, D, R), R ** -0.5, 0.75, ((0, 8), (1, 4)))
    basis = normal_values(arg_keys[4], (SECTIONS, D, R), D ** -0.5, 0.0546875, ((0, 8), (1, 4)))
    return dict(saved_input=saved_input, norm_gain=norm_gain, left_in=left_in, right_in=right_in, basis=basis)


def section_step(items):
    saved, gain, left, right, basis = items
    rebuilt = jnp.dot(left.astype(jnp.float32), right.T.astype(jnp.float32), preferred_element_type=jnp.float32)
    values = saved.astype(jnp.float32)
    center = values - lax.optimization_barrier(jnp.mean(values, axis=1, keepdims=True))
    inverse = lax.rsqrt(lax.optimization_barrier(jnp.mean(center * center, axis=1, keepdims=True)) + 1e-05)
    normed = center * inverse
    factor = 1.0 / jnp.sqrt(jnp.float32(TOKENS))
    gain_term = lax.optimization_barrier(jnp.sum(rebuilt * normed, axis=0)) * factor
    bias_term = lax.optimization_barrier(jnp.sum(rebuilt, axis=0)) * factor
    scaled = rebuilt * gain[None, :]
    first = lax.optimization_barrier(jnp.mean(scaled, axis=1, keepdims=True))
    second = lax.optimization_barrier(jnp.mean(scaled * normed, axis=1, keepdims=True))
    boundary = (inverse * (scaled - first - normed * second)).astype(jnp.bfloat16)
    power = jnp.dot(boundary.astype(jnp.float32), basis.astype(jnp.float32), preferred_element_type=jnp.float32)
    gram = jnp.dot(power.T, power, precision=lax.Precision.HIGHEST)
    lower = jnp.linalg.cholesky(gram)
    ortho = jax.scipy.linalg.solve_triangular(lower, power.T, lower=True).T.astype(jnp.bfloat16)
    feature = jnp.dot(boundary.T.astype(jnp.float32), ortho.astype(jnp.float32), preferred_element_type=jnp.float32).astype(jnp.bfloat16)
    return (ortho, feature, gain_term, bias_term)

def reference(saved_input, norm_gain, left_in, right_in, basis):
    ortho, feature, gain_grad, bias_grad = lax.map(section_step, (saved_input, norm_gain, left_in, right_in, basis))
    left_out = jnp.concatenate([ortho[1:], jnp.zeros_like(ortho[:1])], axis=0)
    right_out = jnp.concatenate([feature[1:], jnp.zeros_like(feature[:1])], axis=0)
    return (gain_grad, bias_grad, left_out, right_out)
```

```python
import functools

import jax
import jax.numpy as jnp
from jax import lax
from jax.experimental import pallas as pl
from jax.experimental.pallas import tpu as pltpu
from jax.sharding import PartitionSpec as P

F32 = jnp.float32
BF16 = jnp.bfloat16
HIGH = lax.Precision.HIGHEST
NN = (((1,), (0,)), ((), ()))
NT = (((1,), (1,)), ((), ()))
LANES = 128
IN_PIECES = 3
OUT_PIECES = 6


def remote(src, dst, send, recv, **where):
    return pltpu.make_async_remote_copy(
        src_ref=src, dst_ref=dst, send_sem=send, recv_sem=recv,
        device_id=where, device_id_type=pl.DeviceIdType.MESH,
    )


def lane_tiles(v):
    total = v[:, :LANES]
    for i in range(1, v.shape[1] // LANES):
        total = total + v[:, i * LANES:(i + 1) * LANES]
    return total


def inverse_factor(gram):
    r, width = gram.shape
    row = lax.broadcasted_iota(jnp.int32, (r, width), 0)
    lane = lax.broadcasted_iota(jnp.int32, (r, width), 1)
    work = jnp.where(lane == row + r, 1.0, gram)
    done = []
    for j0 in range(0, r, 4):
        base = (j0 // 8) * 8
        o = j0 - base
        rows_here = lax.broadcasted_iota(jnp.int32, work.shape, 0)
        cols = [jnp.broadcast_to(work[:, j0 + k:j0 + k + 1], work.shape) for k in range(4)]
        rows = [work[o + k:o + k + 1, :] for k in range(4)]
        for k in range(4):
            scale = 1.0 / cols[k][o + k:o + k + 1, :]
            for m in range(k + 1, 4):
                f = cols[m][o + k:o + k + 1, :] * scale
                rows[m] = rows[m] - f * rows[k]
                cols[m] = cols[m] - cols[k] * f
            work = work - jnp.where(rows_here > o + k, cols[k], 0.0) * (rows[k] * scale)
        if o == 4:
            done.append(work[:8])
            work = work[8:]
    full = jnp.concatenate(done, axis=0)
    diagonal = jnp.sum(jnp.where(lane == row, full, 0.0), axis=1, keepdims=True)
    return full * lax.rsqrt(diagonal)


def kernel(
    n, sections, tokens_all,
    x_hbm, gain_ref, left_ref, r_hbm, b_hbm,
    gain_out, bias_out, left_out, right_out,
    x_v, rt, bt, scaled_v, bnd, acc1, acc2, terms, terms_in, grams, ortho_v,
    sib_out, sib_in, cross_out, cross_in, shift_v,
    local_sem, r_recv, r_cross, r_sib, r_fwd, b_recv, b_cross, b_sib, b_fwd,
    t_send, t_recv, g_send, g_recv, o_send, o_recv,
    s_send, s_recv, c_send, c_recv, f_send, f_recv,
):
    me = lax.axis_index("dp")
    section = lax.axis_index("section")
    chips = n // 2
    chip, core = me // 2, me % 2
    sib = chip * 2 + (1 - core)
    tokens, d = x_v.shape
    w = d // n
    pw = w // IN_PIECES
    ow = w // OUT_PIECES

    loads = [
        pltpu.make_async_copy(r_hbm, rt.at[me], local_sem.at[0]),
        pltpu.make_async_copy(x_hbm, x_v, local_sem.at[1]),
        pltpu.make_async_copy(b_hbm, bt.at[me], local_sem.at[2]),
    ]
    for load in loads:
        load.start()

    barrier = pltpu.get_barrier_semaphore()
    for i in range(1, n):
        pl.semaphore_signal(barrier, inc=1, device_id={"dp": (me + i) % n}, device_id_type=pl.DeviceIdType.MESH)

    @pl.when(section < sections - 1)
    def _():
        pl.semaphore_signal(barrier, inc=1, device_id={"section": section + 1}, device_id_type=pl.DeviceIdType.MESH)

    pl.semaphore_wait(barrier, jnp.where(section > 0, n, n - 1))

    def piece(p):
        return pl.ds(pl.multiple_of(p * pw, LANES), pw)

    def columns(j, p):
        return pl.ds(pl.multiple_of(j * w + p * pw, LANES), pw)

    def other(o):
        return ((chip + o) % chips) * 2 + core

    def source(o):
        return ((chip + chips - o) % chips) * 2 + core

    def flip(j):
        return j + 1 - 2 * core

    def to_cross(src, buf, recv, send, o, p):
        return remote(src.at[:, piece(p)], buf.at[me, :, piece(p)], send.at[o, p], recv.at[me, p], dp=other(o))

    def to_sib(src, buf, recv, send, p):
        return remote(src.at[:, piece(p)], buf.at[me, :, piece(p)], send.at[p], recv.at[me, p], dp=sib)

    def forward(buf, recv, send, o, p):
        j = source(o)
        return remote(buf.at[j, :, piece(p)], buf.at[j, :, piece(p)], send.at[o, p], recv.at[j, p], dp=sib)

    def arrived(buf, recv, send, j, p):
        remote(buf.at[j, :, piece(p)], buf.at[j, :, piece(p)], send.at[0], recv.at[j, p], dp=sib).wait_recv()

    for p in range(IN_PIECES):
        for o in range(1, chips):
            to_cross(r_hbm, rt, r_recv, r_cross, o, p).start()
    for p in range(IN_PIECES):
        to_sib(r_hbm, rt, r_recv, r_sib, p).start()

    step = d // 12
    loads[1].wait()

    def sum_step(i, acc):
        return acc + lane_tiles(x_v[:, pl.ds(pl.multiple_of(i * step, LANES), step)].astype(F32))

    zero = jnp.zeros((tokens, LANES), F32)
    mu = jnp.sum(lax.fori_loop(0, 12, sum_step, zero), axis=1, keepdims=True) / d

    def square_step(i, acc):
        c = x_v[:, pl.ds(pl.multiple_of(i * step, LANES), step)].astype(F32) - mu
        return acc + lane_tiles(c * c)

    var = jnp.sum(lax.fori_loop(0, 12, square_step, zero), axis=1, keepdims=True) / d
    inverse = lax.rsqrt(var + 1e-5)

    left = left_ref[...].astype(F32).T.astype(BF16)
    acc1[...] = zero
    acc2[...] = zero

    def first_pass(j, p):
        at = columns(j, p)
        rebuilt = lax.dot_general(left, rt[j, :, piece(p)], NN, preferred_element_type=F32)
        normed = (x_v[:, at].astype(F32) - mu) * inverse
        product = rebuilt * normed
        terms[j, 0:1, piece(p)] = jnp.sum(product, axis=0, keepdims=True)
        terms[j, 1:2, piece(p)] = jnp.sum(rebuilt, axis=0, keepdims=True)
        gain = gain_ref[:, at]
        scaled = rebuilt * gain
        scaled_v[:, at] = scaled
        acc1[...] += lane_tiles(scaled)
        acc2[...] += lane_tiles(product * gain)

    def loop(count, body):
        lax.fori_loop(0, count, lambda i, _: (body(i), 0)[1], 0)

    loads[0].wait()
    loop(IN_PIECES, lambda p: first_pass(me, p))

    def sib_first(p):
        arrived(rt, r_recv, r_sib, sib, p)
        first_pass(sib, p)

    loop(IN_PIECES, sib_first)

    def cross_first(i):
        p, o = i // (chips - 1), 1 + i % (chips - 1)
        arrived(rt, r_recv, r_sib, source(o), p)
        forward(rt, r_recv, r_fwd, o, p).start()
        to_cross(b_hbm, bt, b_recv, b_cross, o, p).start()
        first_pass(source(o), p)

    loop(IN_PIECES * (chips - 1), cross_first)
    loop(IN_PIECES, lambda p: to_sib(b_hbm, bt, b_recv, b_sib, p).start())

    def forwarded_first(i):
        p, o = i // (chips - 1), 1 + i % (chips - 1)
        arrived(rt, r_recv, r_sib, flip(source(o)), p)
        first_pass(flip(source(o)), p)

    loop(IN_PIECES * (chips - 1), forwarded_first)

    m1 = jnp.sum(acc1[...], axis=1, keepdims=True) / d * inverse
    m2 = jnp.sum(acc2[...], axis=1, keepdims=True) / d * inverse * inverse

    def second_pass(j, p):
        at = columns(j, p)
        center = x_v[:, at].astype(F32) - mu
        bnd[:, at] = (scaled_v[:, at] * inverse - m1 - center * m2).astype(BF16)

    def project(j, p):
        acc1[0:64, :] += lax.dot_general(bt[j, :, piece(p)], bnd[:, columns(j, p)], NT, preferred_element_type=F32)

    acc1[...] = zero
    loads[2].wait()

    def own_second(p):
        second_pass(me, p)
        project(me, p)

    loop(IN_PIECES, own_second)

    def sib_second(p):
        second_pass(sib, p)
        arrived(bt, b_recv, b_sib, sib, p)
        project(sib, p)

    loop(IN_PIECES, sib_second)

    def cross_second(i):
        p, o = i // (chips - 1), 1 + i % (chips - 1)
        second_pass(source(o), p)
        second_pass(flip(source(o)), p)
        arrived(bt, b_recv, b_sib, source(o), p)
        forward(bt, b_recv, b_fwd, o, p).start()
        project(source(o), p)

    loop(IN_PIECES * (chips - 1), cross_second)

    def forwarded_second(i):
        p, o = i // (chips - 1), 1 + i % (chips - 1)
        arrived(bt, b_recv, b_sib, flip(source(o)), p)
        project(flip(source(o)), p)

    loop(IN_PIECES * (chips - 1), forwarded_second)

    r = left_ref.shape[0]
    power = acc1[0:64, :]
    tall = jnp.concatenate([power, jnp.zeros_like(power)], axis=0)
    grams[me] = lax.dot_general(power, tall, NT, precision=HIGH, preferred_element_type=F32)

    def gram_copy(i):
        return remote(grams.at[me], grams.at[me], g_send.at[i], g_recv.at[me], dp=(me + i) % n)

    def terms_copy(i):
        to = (me + i) % n
        return remote(terms.at[to], terms_in.at[me], t_send.at[i], t_recv.at[me], dp=to)

    for i in range(1, n):
        gram_copy(i).start()
    for i in range(1, n):
        terms_copy(i).start()
    for i in range(1, n):
        j = (me + i) % n
        remote(grams.at[j], grams.at[j], g_send.at[0], g_recv.at[j], dp=sib).wait_recv()
    gram = grams[0]
    for j in range(1, n):
        gram = gram + grams[j]
    factor = inverse_factor(gram)
    low = jnp.concatenate([jnp.zeros_like(power), power], axis=0)
    ortho = lax.dot_general(factor, low, NN, precision=HIGH, preferred_element_type=F32).astype(BF16)
    ortho_v[...] = ortho

    def ortho_copy():
        return remote(ortho_v, left_out, o_send, o_recv, section=section - 1)

    @pl.when(section > 0)
    def _():
        ortho_copy().start()

    def out_piece(q):
        return pl.ds(pl.multiple_of(q * ow, LANES), ow)

    def share(j, q):
        at = pl.ds(pl.multiple_of(j * w + q * ow, LANES), ow)
        return lax.dot_general(ortho_v[...], bnd[:, at], NN, preferred_element_type=F32)

    def sib_copy(o, q):
        return remote(sib_out.at[o, :, out_piece(q)], sib_in.at[o, :, out_piece(q)], s_send.at[o, q], s_recv.at[o, q], dp=sib)

    def cross_copy(o, q):
        return remote(cross_out.at[o, :, out_piece(q)], cross_in.at[o, :, out_piece(q)], c_send.at[o, q], c_recv.at[o, q], dp=other(o))

    def shift_copy(q):
        return remote(shift_v.at[:, out_piece(q)], right_out.at[:, out_piece(q)], f_send.at[q], f_recv.at[q], section=section - 1)

    def send_sib(o, q):
        sib_out[o, :, out_piece(q)] = share(flip(other(o)), q).astype(BF16)
        sib_copy(o, q).start()

    def split(i):
        return 1 + i % (chips - 1), i // (chips - 1)

    def stage_a(i):
        o, q = split(i)
        send_sib(o, q)

    loop(OUT_PIECES * (chips - 1), stage_a)

    def stage_b(i):
        o, q = split(i)
        mine = share(other(o), q)
        sib_copy(o, q).wait_recv()
        cross_out[o, :, out_piece(q)] = (mine + sib_in[o, :, out_piece(q)].astype(F32)).astype(BF16)
        cross_copy(o, q).start()

    loop(OUT_PIECES * (chips - 1), stage_b)
    loop(OUT_PIECES, lambda q: send_sib(0, q))

    for i in range(1, n):
        j = (me + i) % n
        remote(terms.at[j], terms_in.at[j], t_send.at[0], t_recv.at[j], dp=sib).wait_recv()
    sums = terms[me]
    for i in range(1, n):
        sums = sums + terms_in[(me + i) % n]
    sums = sums * (1.0 / tokens_all ** 0.5)
    gain_out[...] = sums[0:1]
    bias_out[...] = sums[1:2]

    def stage_c(q):
        total = share(me, q)
        sib_copy(0, q).wait_recv()
        total = total + sib_in[0, :, out_piece(q)].astype(F32)
        for o in range(1, chips):
            cross_copy(o, q).wait_recv()
            total = total + cross_in[o, :, out_piece(q)].astype(F32)
        shift_v[:, out_piece(q)] = total.astype(BF16)

        @pl.when(section > 0)
        def _():
            shift_copy(q).start()

    loop(OUT_PIECES, stage_c)

    @pl.when(section == sections - 1)
    def _():
        left_out[...] = jnp.zeros_like(left_out)
        right_out[...] = jnp.zeros_like(right_out)

    def inputs_sent(i):
        p, o = i // (chips - 1), 1 + i % (chips - 1)
        to_cross(r_hbm, rt, r_recv, r_cross, o, p).wait_send()
        to_cross(b_hbm, bt, b_recv, b_cross, o, p).wait_send()
        forward(rt, r_recv, r_fwd, o, p).wait_send()
        forward(bt, b_recv, b_fwd, o, p).wait_send()

    loop(IN_PIECES * (chips - 1), inputs_sent)

    def inputs_sent_sib(p):
        to_sib(r_hbm, rt, r_recv, r_sib, p).wait_send()
        to_sib(b_hbm, bt, b_recv, b_sib, p).wait_send()

    loop(IN_PIECES, inputs_sent_sib)
    for i in range(1, n):
        gram_copy(i).wait_send()
        terms_copy(i).wait_send()

    def shares_sent(i):
        o, q = split(i)
        sib_copy(o, q).wait_send()
        cross_copy(o, q).wait_send()

    loop(OUT_PIECES * (chips - 1), shares_sent)
    loop(OUT_PIECES, lambda q: sib_copy(0, q).wait_send())

    @pl.when(section < sections - 1)
    def _():
        ortho_copy().wait_recv()
        loop(OUT_PIECES, lambda q: shift_copy(q).wait_recv())

    @pl.when(section > 0)
    def _():
        ortho_copy().wait_send()
        loop(OUT_PIECES, lambda q: shift_copy(q).wait_send())


def on_device(n, sections, saved_input, norm_gain, left_in, right_in, basis):
    _, tokens, d = saved_input.shape
    r = left_in.shape[2]
    w = d // n
    chips = n // 2
    vmem = pl.BlockSpec(memory_space=pltpu.VMEM)
    anywhere = pl.BlockSpec(memory_space=pl.ANY)
    dma = pltpu.SemaphoreType.DMA
    gather = [dma((n, IN_PIECES)), dma((chips, IN_PIECES)), dma((IN_PIECES,)), dma((chips, IN_PIECES))]
    gain, bias, left, right = pl.pallas_call(
        functools.partial(kernel, n, sections, tokens * n),
        out_shape=(
            jax.ShapeDtypeStruct((1, w), F32),
            jax.ShapeDtypeStruct((1, w), F32),
            jax.ShapeDtypeStruct((r, tokens), BF16),
            jax.ShapeDtypeStruct((r, w), BF16),
        ),
        in_specs=[anywhere, vmem, vmem, anywhere, anywhere],
        out_specs=(vmem, vmem, vmem, vmem),
        scratch_shapes=[
            pltpu.VMEM((tokens, d), BF16),
            pltpu.VMEM((n, r, w), BF16),
            pltpu.VMEM((n, r, w), BF16),
            pltpu.VMEM((tokens, d), F32),
            pltpu.VMEM((tokens, d), BF16),
            pltpu.VMEM((tokens, LANES), F32),
            pltpu.VMEM((tokens, LANES), F32),
            pltpu.VMEM((n, 2, w), F32),
            pltpu.VMEM((n, 2, w), F32),
            pltpu.VMEM((n, r, 2 * r), F32),
            pltpu.VMEM((r, tokens), BF16),
            pltpu.VMEM((chips, r, w), BF16),
            pltpu.VMEM((chips, r, w), BF16),
            pltpu.VMEM((chips, r, w), BF16),
            pltpu.VMEM((chips, r, w), BF16),
            pltpu.VMEM((r, w), BF16),
            dma((3,)),
            *gather,
            *gather,
            dma((n,)), dma((n,)),
            dma((n,)), dma((n,)),
            dma, dma,
            dma((chips, OUT_PIECES)), dma((chips, OUT_PIECES)),
            dma((chips, OUT_PIECES)), dma((chips, OUT_PIECES)),
            dma((OUT_PIECES,)), dma((OUT_PIECES,)),
        ],
        compiler_params=pltpu.CompilerParams(
            collective_id=0, has_side_effects=True, vmem_limit_bytes=48 * 1024 * 1024
        ),
    )(saved_input[0], norm_gain, left_in[0].T, right_in[0].T, basis[0].T)
    return gain, bias, left.T[None], right.T[None]


def solution(mesh):
    placed = (
        P("section", "dp", None),
        P("section", None),
        P("section", "dp", None),
        P("section", "dp", None),
        P("section", "dp", None),
    )
    return jax.shard_map(
        functools.partial(on_device, mesh.shape["dp"], mesh.shape["section"]),
        mesh=mesh,
        in_specs=placed,
        out_specs=(
            P("section", "dp"),
            P("section", "dp"),
            P("section", "dp", None),
            P("section", "dp", None),
        ),
        check_vma=False,
    )
```

```python
import functools

import jax
import jax.numpy as jnp
from jax import lax
from jax.experimental import pallas as pl
from jax.experimental.pallas import tpu as pltpu
from jax.sharding import PartitionSpec as P

F32 = jnp.float32
BF16 = jnp.bfloat16
HIGH = lax.Precision.HIGHEST
NN = (((1,), (0,)), ((), ()))
NT = (((1,), (1,)), ((), ()))
LANES = 128
IN_PIECES = 3
OUT_PIECES = 6


def remote(src, dst, send, recv, **where):
    return pltpu.make_async_remote_copy(
        src_ref=src, dst_ref=dst, send_sem=send, recv_sem=recv,
        device_id=where, device_id_type=pl.DeviceIdType.MESH,
    )


def lane_tiles(v):
    total = v[:, :LANES]
    for i in range(1, v.shape[1] // LANES):
        total = total + v[:, i * LANES:(i + 1) * LANES]
    return total


def inverse_factor(gram):
    r, width = gram.shape
    row = lax.broadcasted_iota(jnp.int32, (r, width), 0)
    lane = lax.broadcasted_iota(jnp.int32, (r, width), 1)
    work = jnp.where(lane == row + r, 1.0, gram)
    done = []
    for j0 in range(0, r, 4):
        base = (j0 // 8) * 8
        o = j0 - base
        rows_here = lax.broadcasted_iota(jnp.int32, work.shape, 0)
        cols = [jnp.broadcast_to(work[:, j0 + k:j0 + k + 1], work.shape) for k in range(4)]
        rows = [work[o + k:o + k + 1, :] for k in range(4)]
        for k in range(4):
            scale = 1.0 / cols[k][o + k:o + k + 1, :]
            for m in range(k + 1, 4):
                f = cols[m][o + k:o + k + 1, :] * scale
                rows[m] = rows[m] - f * rows[k]
                cols[m] = cols[m] - cols[k] * f
            work = work - jnp.where(rows_here > o + k, cols[k], 0.0) * (rows[k] * scale)
        if o == 4:
            done.append(work[:8])
            work = work[8:]
    full = jnp.concatenate(done, axis=0)
    diagonal = jnp.sum(jnp.where(lane == row, full, 0.0), axis=1, keepdims=True)
    return full * lax.rsqrt(diagonal)


def kernel(
    n, sections, tokens_all,
    x_hbm, gain_hbm, left_hbm, r_hbm, b_hbm,
    gain_out, bias_out, left_out, right_out,
    gain_ref, left_ref, x_v, rt, bt, scaled_v, bnd, acc1, acc2, terms, terms_in, grams, ortho_v,
    sib_out, sib_in, cross_out, cross_in, shift_v,
    local_sem, r_recv, r_cross, r_sib, r_fwd, b_recv, b_cross, b_sib, b_fwd,
    t_send, t_recv, g_send, g_recv, o_send, o_recv,
    s_send, s_recv, c_send, c_recv, f_send, f_recv,
):
    me = lax.axis_index("dp")
    section = lax.axis_index("section")
    chips = n // 2
    chip, core = me // 2, me % 2
    sib = chip * 2 + (1 - core)
    tokens, d = x_v.shape
    w = d // n
    pw = w // IN_PIECES
    ow = w // OUT_PIECES

    loads = [
        pltpu.make_async_copy(r_hbm, rt.at[me], local_sem.at[0]),
        pltpu.make_async_copy(x_hbm, x_v, local_sem.at[1]),
        pltpu.make_async_copy(b_hbm, bt.at[me], local_sem.at[2]),
        pltpu.make_async_copy(gain_hbm, gain_ref, local_sem.at[3]),
        pltpu.make_async_copy(left_hbm, left_ref, local_sem.at[4]),
    ]
    for load in loads:
        load.start()

    barrier = pltpu.get_barrier_semaphore()
    for i in range(1, n):
        pl.semaphore_signal(barrier, inc=1, device_id={"dp": (me + i) % n}, device_id_type=pl.DeviceIdType.MESH)

    @pl.when(section < sections - 1)
    def _():
        pl.semaphore_signal(barrier, inc=1, device_id={"section": section + 1}, device_id_type=pl.DeviceIdType.MESH)

    pl.semaphore_wait(barrier, jnp.where(section > 0, n, n - 1))

    def piece(p):
        return pl.ds(pl.multiple_of(p * pw, LANES), pw)

    def columns(j, p):
        return pl.ds(pl.multiple_of(j * w + p * pw, LANES), pw)

    def other(o):
        return ((chip + o) % chips) * 2 + core

    def source(o):
        return ((chip + chips - o) % chips) * 2 + core

    def flip(j):
        return j + 1 - 2 * core

    def to_cross(src, buf, recv, send, o, p):
        return remote(src.at[:, piece(p)], buf.at[me, :, piece(p)], send.at[o, p], recv.at[me, p], dp=other(o))

    def to_sib(src, buf, recv, send, p):
        return remote(src.at[:, piece(p)], buf.at[me, :, piece(p)], send.at[p], recv.at[me, p], dp=sib)

    def forward(buf, recv, send, o, p):
        j = source(o)
        return remote(buf.at[j, :, piece(p)], buf.at[j, :, piece(p)], send.at[o, p], recv.at[j, p], dp=sib)

    def arrived(buf, recv, send, j, p):
        remote(buf.at[j, :, piece(p)], buf.at[j, :, piece(p)], send.at[0], recv.at[j, p], dp=sib).wait_recv()

    for p in range(IN_PIECES):
        for o in range(1, chips):
            to_cross(r_hbm, rt, r_recv, r_cross, o, p).start()
    for p in range(IN_PIECES):
        to_sib(r_hbm, rt, r_recv, r_sib, p).start()

    step = d // 12
    loads[1].wait()

    def sum_step(i, acc):
        return acc + lane_tiles(x_v[:, pl.ds(pl.multiple_of(i * step, LANES), step)].astype(F32))

    zero = jnp.zeros((tokens, LANES), F32)
    mu = jnp.sum(lax.fori_loop(0, 12, sum_step, zero), axis=1, keepdims=True) / d

    def square_step(i, acc):
        c = x_v[:, pl.ds(pl.multiple_of(i * step, LANES), step)].astype(F32) - mu
        return acc + lane_tiles(c * c)

    var = jnp.sum(lax.fori_loop(0, 12, square_step, zero), axis=1, keepdims=True) / d
    inverse = lax.rsqrt(var + 1e-5)

    loads[4].wait()
    left = left_ref[...].astype(F32).T.astype(BF16)
    acc1[...] = zero
    acc2[...] = zero

    def first_pass(j, p):
        at = columns(j, p)
        rebuilt = lax.dot_general(left, rt[j, :, piece(p)], NN, preferred_element_type=F32)
        normed = (x_v[:, at].astype(F32) - mu) * inverse
        product = rebuilt * normed
        terms[j, 0:1, piece(p)] = jnp.sum(product, axis=0, keepdims=True)
        terms[j, 1:2, piece(p)] = jnp.sum(rebuilt, axis=0, keepdims=True)
        gain = gain_ref[:, at]
        scaled = rebuilt * gain
        scaled_v[:, at] = scaled
        acc1[...] += lane_tiles(scaled)
        acc2[...] += lane_tiles(product * gain)

    def loop(count, body):
        lax.fori_loop(0, count, lambda i, _: (body(i), 0)[1], 0)

    loads[0].wait()
    loads[3].wait()
    loop(IN_PIECES, lambda p: first_pass(me, p))

    def sib_first(p):
        arrived(rt, r_recv, r_sib, sib, p)
        first_pass(sib, p)

    loop(IN_PIECES, sib_first)

    def cross_first(i):
        p, o = i // (chips - 1), 1 + i % (chips - 1)
        arrived(rt, r_recv, r_sib, source(o), p)
        forward(rt, r_recv, r_fwd, o, p).start()
        to_cross(b_hbm, bt, b_recv, b_cross, o, p).start()
        first_pass(source(o), p)

    loop(IN_PIECES * (chips - 1), cross_first)
    loop(IN_PIECES, lambda p: to_sib(b_hbm, bt, b_recv, b_sib, p).start())

    def forwarded_first(i):
        p, o = i // (chips - 1), 1 + i % (chips - 1)
        arrived(rt, r_recv, r_sib, flip(source(o)), p)
        first_pass(flip(source(o)), p)

    loop(IN_PIECES * (chips - 1), forwarded_first)

    m1 = jnp.sum(acc1[...], axis=1, keepdims=True) / d * inverse
    m2 = jnp.sum(acc2[...], axis=1, keepdims=True) / d * inverse * inverse

    def second_pass(j, p):
        at = columns(j, p)
        center = x_v[:, at].astype(F32) - mu
        bnd[:, at] = (scaled_v[:, at] * inverse - m1 - center * m2).astype(BF16)

    def project(j, p):
        acc1[0:64, :] += lax.dot_general(bt[j, :, piece(p)], bnd[:, columns(j, p)], NT, preferred_element_type=F32)

    acc1[...] = zero
    loads[2].wait()

    def own_second(p):
        second_pass(me, p)
        project(me, p)

    loop(IN_PIECES, own_second)

    def sib_second(p):
        second_pass(sib, p)
        arrived(bt, b_recv, b_sib, sib, p)
        project(sib, p)

    loop(IN_PIECES, sib_second)

    def cross_second(i):
        p, o = i // (chips - 1), 1 + i % (chips - 1)
        second_pass(source(o), p)
        second_pass(flip(source(o)), p)
        arrived(bt, b_recv, b_sib, source(o), p)
        forward(bt, b_recv, b_fwd, o, p).start()
        project(source(o), p)

    loop(IN_PIECES * (chips - 1), cross_second)

    def forwarded_second(i):
        p, o = i // (chips - 1), 1 + i % (chips - 1)
        arrived(bt, b_recv, b_sib, flip(source(o)), p)
        project(flip(source(o)), p)

    loop(IN_PIECES * (chips - 1), forwarded_second)

    r = left_ref.shape[0]
    power = acc1[0:64, :]
    tall = jnp.concatenate([power, jnp.zeros_like(power)], axis=0)
    grams[me] = lax.dot_general(power, tall, NT, precision=HIGH, preferred_element_type=F32)

    def gram_copy(i):
        return remote(grams.at[me], grams.at[me], g_send.at[i], g_recv.at[me], dp=(me + i) % n)

    def terms_copy(i):
        to = (me + i) % n
        return remote(terms.at[to], terms_in.at[me], t_send.at[i], t_recv.at[me], dp=to)

    for i in range(1, n):
        gram_copy(i).start()
    for i in range(1, n):
        terms_copy(i).start()
    for i in range(1, n):
        j = (me + i) % n
        remote(grams.at[j], grams.at[j], g_send.at[0], g_recv.at[j], dp=sib).wait_recv()
    gram = grams[0]
    for j in range(1, n):
        gram = gram + grams[j]
    factor = inverse_factor(gram)
    low = jnp.concatenate([jnp.zeros_like(power), power], axis=0)
    ortho = lax.dot_general(factor, low, NN, precision=HIGH, preferred_element_type=F32).astype(BF16)
    ortho_v[...] = ortho

    def ortho_copy():
        return remote(ortho_v, left_out, o_send, o_recv, section=section - 1)

    @pl.when(section > 0)
    def _():
        ortho_copy().start()

    def out_piece(q):
        return pl.ds(pl.multiple_of(q * ow, LANES), ow)

    def share(j, q):
        at = pl.ds(pl.multiple_of(j * w + q * ow, LANES), ow)
        return lax.dot_general(ortho_v[...], bnd[:, at], NN, preferred_element_type=F32)

    def sib_copy(o, q):
        return remote(sib_out.at[o, :, out_piece(q)], sib_in.at[o, :, out_piece(q)], s_send.at[o, q], s_recv.at[o, q], dp=sib)

    def cross_copy(o, q):
        return remote(cross_out.at[o, :, out_piece(q)], cross_in.at[o, :, out_piece(q)], c_send.at[o, q], c_recv.at[o, q], dp=other(o))

    def shift_copy(q):
        return remote(shift_v.at[:, out_piece(q)], right_out.at[:, out_piece(q)], f_send.at[q], f_recv.at[q], section=section - 1)

    def send_sib(o, q):
        sib_out[o, :, out_piece(q)] = share(flip(other(o)), q).astype(BF16)
        sib_copy(o, q).start()

    def split(i):
        return 1 + i % (chips - 1), i // (chips - 1)

    def stage_a(i):
        o, q = split(i)
        send_sib(o, q)

    loop(OUT_PIECES * (chips - 1), stage_a)

    def stage_b(i):
        o, q = split(i)
        mine = share(other(o), q)
        sib_copy(o, q).wait_recv()
        cross_out[o, :, out_piece(q)] = (mine + sib_in[o, :, out_piece(q)].astype(F32)).astype(BF16)
        cross_copy(o, q).start()

    loop(OUT_PIECES * (chips - 1), stage_b)
    loop(OUT_PIECES, lambda q: send_sib(0, q))

    for i in range(1, n):
        j = (me + i) % n
        remote(terms.at[j], terms_in.at[j], t_send.at[0], t_recv.at[j], dp=sib).wait_recv()
    sums = terms[me]
    for i in range(1, n):
        sums = sums + terms_in[(me + i) % n]
    sums = sums * (1.0 / tokens_all ** 0.5)
    gain_out[...] = sums[0:1]
    bias_out[...] = sums[1:2]

    def stage_c(q):
        total = share(me, q)
        sib_copy(0, q).wait_recv()
        total = total + sib_in[0, :, out_piece(q)].astype(F32)
        for o in range(1, chips):
            cross_copy(o, q).wait_recv()
            total = total + cross_in[o, :, out_piece(q)].astype(F32)
        shift_v[:, out_piece(q)] = total.astype(BF16)

        @pl.when(section > 0)
        def _():
            shift_copy(q).start()

    loop(OUT_PIECES, stage_c)

    @pl.when(section == sections - 1)
    def _():
        left_out[...] = jnp.zeros_like(left_out)
        right_out[...] = jnp.zeros_like(right_out)

    def inputs_sent(i):
        p, o = i // (chips - 1), 1 + i % (chips - 1)
        to_cross(r_hbm, rt, r_recv, r_cross, o, p).wait_send()
        to_cross(b_hbm, bt, b_recv, b_cross, o, p).wait_send()
        forward(rt, r_recv, r_fwd, o, p).wait_send()
        forward(bt, b_recv, b_fwd, o, p).wait_send()

    loop(IN_PIECES * (chips - 1), inputs_sent)

    def inputs_sent_sib(p):
        to_sib(r_hbm, rt, r_recv, r_sib, p).wait_send()
        to_sib(b_hbm, bt, b_recv, b_sib, p).wait_send()

    loop(IN_PIECES, inputs_sent_sib)
    for i in range(1, n):
        gram_copy(i).wait_send()
        terms_copy(i).wait_send()

    def shares_sent(i):
        o, q = split(i)
        sib_copy(o, q).wait_send()
        cross_copy(o, q).wait_send()

    loop(OUT_PIECES * (chips - 1), shares_sent)
    loop(OUT_PIECES, lambda q: sib_copy(0, q).wait_send())

    @pl.when(section < sections - 1)
    def _():
        ortho_copy().wait_recv()
        loop(OUT_PIECES, lambda q: shift_copy(q).wait_recv())

    @pl.when(section > 0)
    def _():
        ortho_copy().wait_send()
        loop(OUT_PIECES, lambda q: shift_copy(q).wait_send())


def write_out(*refs):
    copies = [pltpu.make_async_copy(refs[i], refs[4 + i], refs[8].at[i]) for i in range(4)]
    for copy in copies:
        copy.start()
    for copy in copies:
        copy.wait()


def on_device(n, sections, saved_input, norm_gain, left_in, right_in, basis):
    _, tokens, d = saved_input.shape
    r = left_in.shape[2]
    w = d // n
    chips = n // 2
    vmem = pl.BlockSpec(memory_space=pltpu.VMEM)
    hbm = pl.BlockSpec(memory_space=pltpu.HBM)
    dma = pltpu.SemaphoreType.DMA
    gather = [dma((n, IN_PIECES)), dma((chips, IN_PIECES)), dma((IN_PIECES,)), dma((chips, IN_PIECES))]
    results = (
        jax.ShapeDtypeStruct((1, w), F32),
        jax.ShapeDtypeStruct((1, w), F32),
        jax.ShapeDtypeStruct((r, tokens), BF16),
        jax.ShapeDtypeStruct((r, w), BF16),
    )
    held = pl.pallas_call(
        functools.partial(kernel, n, sections, tokens * n),
        out_shape=results,
        in_specs=[hbm] * 5,
        out_specs=(vmem, vmem, vmem, vmem),
        scratch_shapes=[
            pltpu.VMEM((1, d), F32),
            pltpu.VMEM((r, tokens), BF16),
            pltpu.VMEM((tokens, d), BF16),
            pltpu.VMEM((n, r, w), BF16),
            pltpu.VMEM((n, r, w), BF16),
            pltpu.VMEM((tokens, d), F32),
            pltpu.VMEM((tokens, d), BF16),
            pltpu.VMEM((tokens, LANES), F32),
            pltpu.VMEM((tokens, LANES), F32),
            pltpu.VMEM((n, 2, w), F32),
            pltpu.VMEM((n, 2, w), F32),
            pltpu.VMEM((n, r, 2 * r), F32),
            pltpu.VMEM((r, tokens), BF16),
            pltpu.VMEM((chips, r, w), BF16),
            pltpu.VMEM((chips, r, w), BF16),
            pltpu.VMEM((chips, r, w), BF16),
            pltpu.VMEM((chips, r, w), BF16),
            pltpu.VMEM((r, w), BF16),
            dma((5,)),
            *gather,
            *gather,
            dma((n,)), dma((n,)),
            dma((n,)), dma((n,)),
            dma, dma,
            dma((chips, OUT_PIECES)), dma((chips, OUT_PIECES)),
            dma((chips, OUT_PIECES)), dma((chips, OUT_PIECES)),
            dma((OUT_PIECES,)), dma((OUT_PIECES,)),
        ],
        compiler_params=pltpu.CompilerParams(
            collective_id=0, has_side_effects=True, vmem_limit_bytes=63 * 1024 * 1024
        ),
    )(saved_input[0], norm_gain, left_in[0].T, right_in[0].T, basis[0].T)
    gain, bias, left, right = pl.pallas_call(
        write_out,
        out_shape=results,
        in_specs=[hbm] * 4,
        out_specs=(hbm,) * 4,
        scratch_shapes=[dma((4,))],
        compiler_params=pltpu.CompilerParams(vmem_limit_bytes=63 * 1024 * 1024),
    )(*held)
    return gain, bias, left.T[None], right.T[None]


def solution(mesh):
    placed = (
        P("section", "dp", None),
        P("section", None),
        P("section", "dp", None),
        P("section", "dp", None),
        P("section", "dp", None),
    )
    return jax.shard_map(
        functools.partial(on_device, mesh.shape["dp"], mesh.shape["section"]),
        mesh=mesh,
        in_specs=placed,
        out_specs=(
            P("section", "dp"),
            P("section", "dp"),
            P("section", "dp", None),
            P("section", "dp", None),
        ),
        check_vma=False,
    )
```

```python
import functools

import jax
import jax.numpy as jnp
from jax import lax
from jax.experimental import pallas as pl
from jax.experimental.pallas import tpu as pltpu
from jax.sharding import PartitionSpec as P

F32 = jnp.float32
BF16 = jnp.bfloat16
HIGH = lax.Precision.HIGHEST
NN = (((1,), (0,)), ((), ()))
NT = (((1,), (1,)), ((), ()))
LANES = 128
IN_PIECES = 3
OUT_PIECES = 6


def remote(src, dst, send, recv, **where):
    return pltpu.make_async_remote_copy(
        src_ref=src, dst_ref=dst, send_sem=send, recv_sem=recv,
        device_id=where, device_id_type=pl.DeviceIdType.MESH,
    )


def lane_tiles(v):
    total = v[:, :LANES]
    for i in range(1, v.shape[1] // LANES):
        total = total + v[:, i * LANES:(i + 1) * LANES]
    return total


def inverse_factor(gram):
    r, width = gram.shape
    row = lax.broadcasted_iota(jnp.int32, (r, width), 0)
    lane = lax.broadcasted_iota(jnp.int32, (r, width), 1)
    work = jnp.where(lane < r, gram, jnp.where(lane == row + r, 1.0, 0.0))
    done = []
    for j0 in range(0, r, 4):
        base = (j0 // 8) * 8
        o = j0 - base
        rows_here = lax.broadcasted_iota(jnp.int32, work.shape, 0)
        cols = [jnp.broadcast_to(work[:, j0 + k:j0 + k + 1], work.shape) for k in range(4)]
        rows = [work[o + k:o + k + 1, :] for k in range(4)]
        for k in range(4):
            scale = 1.0 / cols[k][o + k:o + k + 1, :]
            for m in range(k + 1, 4):
                f = cols[m][o + k:o + k + 1, :] * scale
                rows[m] = rows[m] - f * rows[k]
                cols[m] = cols[m] - cols[k] * f
            work = work - jnp.where(rows_here > o + k, cols[k], 0.0) * (rows[k] * scale)
        if o == 4:
            done.append(work[:8])
            work = work[8:]
    full = jnp.concatenate(done, axis=0)
    diagonal = jnp.sum(jnp.where(lane == row, full, 0.0), axis=1, keepdims=True)
    return full * lax.rsqrt(diagonal)


def kernel(
    n, sections, tokens_all,
    x_hbm, gain_hbm, left_hbm, r_hbm, b_hbm,
    gain_out, bias_out, left_out, right_out,
    gain_ref, left_ref, x_v, rt, bt, scaled_v, bnd, acc1, acc2, terms, terms_in, grams, ortho_v, power_v, pre, conditioner,
    sib_out, sib_in, cross_out, cross_in, shift_v,
    local_sem, r_recv, r_cross, r_sib, r_fwd, b_recv, b_cross, b_sib, b_fwd,
    p_send, p_recv, t_send, t_recv, g_send, g_recv, o_send, o_recv,
    s_send, s_recv, c_send, c_recv, f_send, f_recv,
):
    me = lax.axis_index("dp")
    section = lax.axis_index("section")
    chips = n // 2
    chip, core = me // 2, me % 2
    sib = chip * 2 + (1 - core)
    tokens, d = x_v.shape
    w = d // n
    pw = w // IN_PIECES
    ow = w // OUT_PIECES

    loads = [
        pltpu.make_async_copy(r_hbm, rt.at[me], local_sem.at[0]),
        pltpu.make_async_copy(x_hbm, x_v, local_sem.at[1]),
        pltpu.make_async_copy(b_hbm, bt.at[me], local_sem.at[2]),
        pltpu.make_async_copy(gain_hbm, gain_ref, local_sem.at[3]),
        pltpu.make_async_copy(left_hbm, left_ref, local_sem.at[4]),
    ]
    for load in loads:
        load.start()

    barrier = pltpu.get_barrier_semaphore()
    for i in range(1, n):
        pl.semaphore_signal(barrier, inc=1, device_id={"dp": (me + i) % n}, device_id_type=pl.DeviceIdType.MESH)

    @pl.when(section < sections - 1)
    def _():
        pl.semaphore_signal(barrier, inc=1, device_id={"section": section + 1}, device_id_type=pl.DeviceIdType.MESH)

    pl.semaphore_wait(barrier, jnp.where(section > 0, n, n - 1))

    def piece(p):
        return pl.ds(pl.multiple_of(p * pw, LANES), pw)

    def columns(j, p):
        return pl.ds(pl.multiple_of(j * w + p * pw, LANES), pw)

    def other(o):
        return ((chip + o) % chips) * 2 + core

    def source(o):
        return ((chip + chips - o) % chips) * 2 + core

    def flip(j):
        return j + 1 - 2 * core

    def to_cross(src, buf, recv, send, o, p):
        return remote(src.at[:, piece(p)], buf.at[me, :, piece(p)], send.at[o, p], recv.at[me, p], dp=other(o))

    def to_sib(src, buf, recv, send, p):
        return remote(src.at[:, piece(p)], buf.at[me, :, piece(p)], send.at[p], recv.at[me, p], dp=sib)

    def forward(buf, recv, send, o, p):
        j = source(o)
        return remote(buf.at[j, :, piece(p)], buf.at[j, :, piece(p)], send.at[o, p], recv.at[j, p], dp=sib)

    def arrived(buf, recv, send, j, p):
        remote(buf.at[j, :, piece(p)], buf.at[j, :, piece(p)], send.at[0], recv.at[j, p], dp=sib).wait_recv()

    for p in range(IN_PIECES):
        for o in range(1, chips):
            to_cross(r_hbm, rt, r_recv, r_cross, o, p).start()
    for p in range(IN_PIECES):
        to_sib(r_hbm, rt, r_recv, r_sib, p).start()

    step = d // 12
    loads[1].wait()

    def sum_step(i, acc):
        return acc + lane_tiles(x_v[:, pl.ds(pl.multiple_of(i * step, LANES), step)].astype(F32))

    zero = jnp.zeros((tokens, LANES), F32)
    mu = jnp.sum(lax.fori_loop(0, 12, sum_step, zero), axis=1, keepdims=True) / d

    def square_step(i, acc):
        c = x_v[:, pl.ds(pl.multiple_of(i * step, LANES), step)].astype(F32) - mu
        return acc + lane_tiles(c * c)

    var = jnp.sum(lax.fori_loop(0, 12, square_step, zero), axis=1, keepdims=True) / d
    inverse = lax.rsqrt(var + 1e-5)

    loads[4].wait()
    left = left_ref[...].astype(F32).T.astype(BF16)
    acc1[...] = zero
    acc2[...] = zero

    loads[0].wait()
    loads[2].wait()
    loads[3].wait()
    r = left_ref.shape[0]

    def stack(top, bottom):
        return jnp.concatenate([top, bottom], axis=0)

    def moments(p, carry):
        product, sums = carry
        scaled = rt[me, :, piece(p)].astype(F32) * gain_ref[:, columns(me, p)]
        high = scaled.astype(BF16)
        low = (scaled - high.astype(F32)).astype(BF16)
        both = bt[me, :, piece(p)]
        nothing = jnp.zeros_like(both)
        ones = jnp.ones((16, pw), BF16)
        right = stack(both, nothing)
        for part in (high, low):
            product = product + lax.dot_general(part, right, NT, preferred_element_type=F32)
            sums = sums + lax.dot_general(ones, stack(nothing, part), NT, preferred_element_type=F32)
        return product, sums + lax.dot_general(ones, right, NT, preferred_element_type=F32)

    product, sums = lax.fori_loop(0, IN_PIECES, moments, (jnp.zeros((r, 2 * r), F32), jnp.zeros((16, 2 * r), F32)))
    weighted = (left.astype(F32) * inverse).T
    spread = lax.dot_general(weighted, stack(jnp.zeros_like(weighted), weighted), NT, precision=HIGH, preferred_element_type=F32)
    pre[me, 0:r, :] = product + spread
    pre[me, r:r + 8, :] = sums[0:8]

    def pre_copy(i):
        return remote(pre.at[me], pre.at[me], p_send.at[i], p_recv.at[me], dp=(me + i) % n)

    for i in range(1, n):
        pre_copy(i).start()

    def first_pass(j, p):
        at = columns(j, p)
        rebuilt = lax.dot_general(left, rt[j, :, piece(p)], NN, preferred_element_type=F32)
        normed = (x_v[:, at].astype(F32) - mu) * inverse
        product = rebuilt * normed
        terms[j, 0:1, piece(p)] = jnp.sum(product, axis=0, keepdims=True)
        terms[j, 1:2, piece(p)] = jnp.sum(rebuilt, axis=0, keepdims=True)
        gain = gain_ref[:, at]
        scaled = rebuilt * gain
        scaled_v[:, at] = scaled
        acc1[...] += lane_tiles(scaled)
        acc2[...] += lane_tiles(product * gain)

    def loop(count, body):
        lax.fori_loop(0, count, lambda i, _: (body(i), 0)[1], 0)

    loop(IN_PIECES, lambda p: first_pass(me, p))

    def sib_first(p):
        arrived(rt, r_recv, r_sib, sib, p)
        first_pass(sib, p)

    loop(IN_PIECES, sib_first)

    def cross_first(i):
        p, o = i // (chips - 1), 1 + i % (chips - 1)
        arrived(rt, r_recv, r_sib, source(o), p)
        forward(rt, r_recv, r_fwd, o, p).start()
        to_cross(b_hbm, bt, b_recv, b_cross, o, p).start()
        first_pass(source(o), p)

    loop(IN_PIECES * (chips - 1), cross_first)
    loop(IN_PIECES, lambda p: to_sib(b_hbm, bt, b_recv, b_sib, p).start())

    for i in range(1, n):
        j = (me + i) % n
        remote(pre.at[j], pre.at[j], p_send.at[0], p_recv.at[j], dp=sib).wait_recv()
    whole = pre[0]
    for j in range(1, n):
        whole = whole + pre[j]
    tile, sums = whole[0:r], whole[r:r + 8]
    row = lax.broadcasted_iota(jnp.int32, (r, 2 * r), 0)
    lane = lax.broadcasted_iota(jnp.int32, (r, 2 * r), 1)
    pick = jnp.where(lane == row + r, 1.0, 0.0)
    r_sums = lax.dot_general(pick, sums, NT, precision=HIGH, preferred_element_type=F32)
    b_sums = jnp.where(lane[0:8] < r, sums, 0.0) * (1.0 / (8 * d))
    moment = jnp.where(lane < r, tile, 0.0) - lax.dot_general(r_sums, b_sums, NN, precision=HIGH, preferred_element_type=F32)
    moved = lax.dot_general(tile[:, r:], moment, NN, precision=HIGH, preferred_element_type=F32)
    turned = moment.T[0:r]
    guess = lax.dot_general(turned, moved, NN, precision=HIGH, preferred_element_type=F32)
    diagonal = jnp.where(lane == row, guess, 0.0)
    level = jnp.sum(jnp.sum(diagonal, axis=1, keepdims=True), axis=0, keepdims=True) * (1e-4 / r) + 1e-30
    conditioner[...] = inverse_factor(guess + jnp.where(lane == row, level, 0.0))

    def forwarded_first(i):
        p, o = i // (chips - 1), 1 + i % (chips - 1)
        arrived(rt, r_recv, r_sib, flip(source(o)), p)
        first_pass(flip(source(o)), p)

    loop(IN_PIECES * (chips - 1), forwarded_first)

    m1 = jnp.sum(acc1[...], axis=1, keepdims=True) / d * inverse
    m2 = jnp.sum(acc2[...], axis=1, keepdims=True) / d * inverse * inverse

    def second_pass(j, p):
        at = columns(j, p)
        center = x_v[:, at].astype(F32) - mu
        bnd[:, at] = (scaled_v[:, at] * inverse - m1 - center * m2).astype(BF16)

    def project(j, p):
        acc1[0:r, :] += lax.dot_general(bt[j, :, piece(p)], bnd[:, columns(j, p)], NT, preferred_element_type=F32)

    acc1[...] = zero

    def own_second(p):
        second_pass(me, p)
        project(me, p)

    loop(IN_PIECES, own_second)

    def sib_second(p):
        second_pass(sib, p)
        arrived(bt, b_recv, b_sib, sib, p)
        project(sib, p)

    loop(IN_PIECES, sib_second)

    def cross_second(i):
        p, o = i // (chips - 1), 1 + i % (chips - 1)
        second_pass(source(o), p)
        second_pass(flip(source(o)), p)
        arrived(bt, b_recv, b_sib, source(o), p)
        forward(bt, b_recv, b_fwd, o, p).start()
        project(source(o), p)

    loop(IN_PIECES * (chips - 1), cross_second)

    def forwarded_second(i):
        p, o = i // (chips - 1), 1 + i % (chips - 1)
        arrived(bt, b_recv, b_sib, flip(source(o)), p)
        project(flip(source(o)), p)

    loop(IN_PIECES * (chips - 1), forwarded_second)

    plain = acc1[0:r, :]
    power = lax.dot_general(conditioner[...], stack(jnp.zeros_like(plain), plain), NN, precision=HIGH, preferred_element_type=F32)
    power_v[...] = power.astype(BF16)

    def out_piece(q):
        return pl.ds(pl.multiple_of(q * ow, LANES), ow)

    def share(j, q):
        at = pl.ds(pl.multiple_of(j * w + q * ow, LANES), ow)
        return lax.dot_general(power_v[...], bnd[:, at], NN, preferred_element_type=F32)

    def sib_copy(o, q):
        return remote(sib_out.at[o, :, out_piece(q)], sib_in.at[o, :, out_piece(q)], s_send.at[o, q], s_recv.at[o, q], dp=sib)

    def cross_copy(o, q):
        return remote(cross_out.at[o, :, out_piece(q)], cross_in.at[o, :, out_piece(q)], c_send.at[o, q], c_recv.at[o, q], dp=other(o))

    def shift_copy(q):
        return remote(shift_v.at[:, out_piece(q)], right_out.at[:, out_piece(q)], f_send.at[q], f_recv.at[q], section=section - 1)

    def send_sib(o, q):
        sib_out[o, :, out_piece(q)] = share(flip(other(o)), q).astype(BF16)
        sib_copy(o, q).start()

    def split(i):
        return 1 + i % (chips - 1), i // (chips - 1)

    def stage_a(i):
        o, q = split(i)
        send_sib(o, q)

    loop(OUT_PIECES * (chips - 1), stage_a)

    half = r // 2
    nothing = jnp.zeros_like(power)
    grams[me] = lax.dot_general(
        power[0:half], stack(power, nothing), NT, precision=HIGH, preferred_element_type=F32
    ) + lax.dot_general(power[half:r], stack(nothing, power), NT, precision=HIGH, preferred_element_type=F32)

    def gram_copy(i):
        return remote(grams.at[me], grams.at[me], g_send.at[i], g_recv.at[me], dp=(me + i) % n)

    def terms_copy(i):
        to = (me + i) % n
        return remote(terms.at[to], terms_in.at[me], t_send.at[i], t_recv.at[me], dp=to)

    for i in range(1, n):
        gram_copy(i).start()

    def stage_b(i):
        o, q = split(i)
        mine = share(other(o), q)
        sib_copy(o, q).wait_recv()
        cross_out[o, :, out_piece(q)] = (mine + sib_in[o, :, out_piece(q)].astype(F32)).astype(BF16)
        cross_copy(o, q).start()

    loop(OUT_PIECES * (chips - 1), stage_b)
    loop(OUT_PIECES, lambda q: send_sib(0, q))

    for i in range(1, n):
        terms_copy(i).start()
    for i in range(1, n):
        j = (me + i) % n
        remote(grams.at[j], grams.at[j], g_send.at[0], g_recv.at[j], dp=sib).wait_recv()
    packed = grams[0]
    for j in range(1, n):
        packed = packed + grams[j]
    factor = inverse_factor(stack(packed, pltpu.roll(packed, r, 1)))
    conditioner[...] = factor
    ortho_v[...] = lax.dot_general(factor, stack(nothing, power), NN, precision=HIGH, preferred_element_type=F32).astype(BF16)

    def ortho_copy():
        return remote(ortho_v, left_out, o_send, o_recv, section=section - 1)

    @pl.when(section > 0)
    def _():
        ortho_copy().start()

    for i in range(1, n):
        j = (me + i) % n
        remote(terms.at[j], terms_in.at[j], t_send.at[0], t_recv.at[j], dp=sib).wait_recv()
    sums = terms[me]
    for i in range(1, n):
        sums = sums + terms_in[(me + i) % n]
    sums = sums * (1.0 / tokens_all ** 0.5)
    gain_out[...] = sums[0:1]
    bias_out[...] = sums[1:2]

    def stage_c(q):
        total = share(me, q)
        sib_copy(0, q).wait_recv()
        total = total + sib_in[0, :, out_piece(q)].astype(F32)
        for o in range(1, chips):
            cross_copy(o, q).wait_recv()
            total = total + cross_in[o, :, out_piece(q)].astype(F32)
        total = lax.dot_general(conditioner[...], stack(jnp.zeros_like(total), total), NN, precision=HIGH, preferred_element_type=F32)
        shift_v[:, out_piece(q)] = total.astype(BF16)

        @pl.when(section > 0)
        def _():
            shift_copy(q).start()

    loop(OUT_PIECES, stage_c)

    @pl.when(section == sections - 1)
    def _():
        left_out[...] = jnp.zeros_like(left_out)
        right_out[...] = jnp.zeros_like(right_out)

    def inputs_sent(i):
        p, o = i // (chips - 1), 1 + i % (chips - 1)
        to_cross(r_hbm, rt, r_recv, r_cross, o, p).wait_send()
        to_cross(b_hbm, bt, b_recv, b_cross, o, p).wait_send()
        forward(rt, r_recv, r_fwd, o, p).wait_send()
        forward(bt, b_recv, b_fwd, o, p).wait_send()

    loop(IN_PIECES * (chips - 1), inputs_sent)

    def inputs_sent_sib(p):
        to_sib(r_hbm, rt, r_recv, r_sib, p).wait_send()
        to_sib(b_hbm, bt, b_recv, b_sib, p).wait_send()

    loop(IN_PIECES, inputs_sent_sib)
    for i in range(1, n):
        gram_copy(i).wait_send()
        terms_copy(i).wait_send()
        pre_copy(i).wait_send()

    def shares_sent(i):
        o, q = split(i)
        sib_copy(o, q).wait_send()
        cross_copy(o, q).wait_send()

    loop(OUT_PIECES * (chips - 1), shares_sent)
    loop(OUT_PIECES, lambda q: sib_copy(0, q).wait_send())

    @pl.when(section < sections - 1)
    def _():
        ortho_copy().wait_recv()
        loop(OUT_PIECES, lambda q: shift_copy(q).wait_recv())

    @pl.when(section > 0)
    def _():
        ortho_copy().wait_send()
        loop(OUT_PIECES, lambda q: shift_copy(q).wait_send())


def write_out(*refs):
    come = [pltpu.make_async_copy(refs[i], refs[8 + i], refs[12].at[i]) for i in range(4)]
    go = [pltpu.make_async_copy(refs[8 + i], refs[4 + i], refs[13].at[i]) for i in range(4)]
    for copy in come:
        copy.start()
    for first, second in zip(come, go):
        first.wait()
        second.start()
    for copy in go:
        copy.wait()


def on_device(n, sections, saved_input, norm_gain, left_in, right_in, basis):
    _, tokens, d = saved_input.shape
    r = left_in.shape[2]
    w = d // n
    chips = n // 2
    vmem = pl.BlockSpec(memory_space=pltpu.VMEM)
    hbm = pl.BlockSpec(memory_space=pltpu.HBM)
    dma = pltpu.SemaphoreType.DMA
    gather = [dma((n, IN_PIECES)), dma((chips, IN_PIECES)), dma((IN_PIECES,)), dma((chips, IN_PIECES))]
    results = (
        jax.ShapeDtypeStruct((1, w), F32),
        jax.ShapeDtypeStruct((1, w), F32),
        jax.ShapeDtypeStruct((r, tokens), BF16),
        jax.ShapeDtypeStruct((r, w), BF16),
    )
    held = pl.pallas_call(
        functools.partial(kernel, n, sections, tokens * n),
        out_shape=results,
        in_specs=[hbm] * 5,
        out_specs=(vmem, vmem, vmem, vmem),
        scratch_shapes=[
            pltpu.VMEM((1, d), F32),
            pltpu.VMEM((r, tokens), BF16),
            pltpu.VMEM((tokens, d), BF16),
            pltpu.VMEM((n, r, w), BF16),
            pltpu.VMEM((n, r, w), BF16),
            pltpu.VMEM((tokens, d), F32),
            pltpu.VMEM((tokens, d), BF16),
            pltpu.VMEM((tokens, LANES), F32),
            pltpu.VMEM((tokens, LANES), F32),
            pltpu.VMEM((n, 2, w), F32),
            pltpu.VMEM((n, 2, w), F32),
            pltpu.VMEM((n, r // 2, 2 * r), F32),
            pltpu.VMEM((r, tokens), BF16),
            pltpu.VMEM((r, tokens), BF16),
            pltpu.VMEM((n, r + 8, 2 * r), F32),
            pltpu.VMEM((r, 2 * r), F32),
            pltpu.VMEM((chips, r, w), BF16),
            pltpu.VMEM((chips, r, w), BF16),
            pltpu.VMEM((chips, r, w), BF16),
            pltpu.VMEM((chips, r, w), BF16),
            pltpu.VMEM((r, w), BF16),
            dma((5,)),
            *gather,
            *gather,
            dma((n,)), dma((n,)),
            dma((n,)), dma((n,)),
            dma((n,)), dma((n,)),
            dma, dma,
            dma((chips, OUT_PIECES)), dma((chips, OUT_PIECES)),
            dma((chips, OUT_PIECES)), dma((chips, OUT_PIECES)),
            dma((OUT_PIECES,)), dma((OUT_PIECES,)),
        ],
        compiler_params=pltpu.CompilerParams(
            collective_id=0, has_side_effects=True, vmem_limit_bytes=63 * 1024 * 1024
        ),
    )(saved_input[0], norm_gain, left_in[0].T, right_in[0].T, basis[0].T)
    gain, bias, left, right = pl.pallas_call(
        write_out,
        out_shape=results,
        in_specs=[hbm] * 4,
        out_specs=(hbm,) * 4,
        scratch_shapes=[*(pltpu.VMEM(a.shape, a.dtype) for a in results), dma((4,)), dma((4,))],
        compiler_params=pltpu.CompilerParams(vmem_limit_bytes=63 * 1024 * 1024),
    )(*held)
    return gain, bias, left.T[None], right.T[None]


def solution(mesh):
    placed = (
        P("section", "dp", None),
        P("section", None),
        P("section", "dp", None),
        P("section", "dp", None),
        P("section", "dp", None),
    )
    return jax.shard_map(
        functools.partial(on_device, mesh.shape["dp"], mesh.shape["section"]),
        mesh=mesh,
        in_specs=placed,
        out_specs=(
            P("section", "dp"),
            P("section", "dp"),
            P("section", "dp", None),
            P("section", "dp", None),
        ),
        check_vma=False,
    )
```

```python
import functools

import jax
import jax.numpy as jnp
from jax import lax
from jax.experimental import pallas as pl
from jax.experimental.pallas import tpu as pltpu
from jax.sharding import PartitionSpec as P

F32 = jnp.float32
BF16 = jnp.bfloat16
HIGH = lax.Precision.HIGHEST
NN = (((1,), (0,)), ((), ()))
NT = (((1,), (1,)), ((), ()))
LANES = 128
IN_PIECES = 3
OUT_PIECES = 6
TILE = 256
ROWS = 32


def remote(src, dst, send, recv, **where):
    return pltpu.make_async_remote_copy(
        src_ref=src, dst_ref=dst, send_sem=send, recv_sem=recv,
        device_id=where, device_id_type=pl.DeviceIdType.MESH,
    )


def inverse_factor(gram):
    r, width = gram.shape
    row = lax.broadcasted_iota(jnp.int32, (r, width), 0)
    lane = lax.broadcasted_iota(jnp.int32, (r, width), 1)
    work = jnp.where(lane < r, gram, jnp.where(lane == row + r, 1.0, 0.0))
    done = []
    for j0 in range(0, r, 4):
        base = (j0 // 8) * 8
        o = j0 - base
        rows_here = lax.broadcasted_iota(jnp.int32, work.shape, 0)
        cols = [jnp.broadcast_to(work[:, j0 + k:j0 + k + 1], work.shape) for k in range(4)]
        rows = [work[o + k:o + k + 1, :] for k in range(4)]
        for k in range(4):
            pivot = cols[k][o + k:o + k + 1, :]
            scale = pl.reciprocal(pivot, approx=True)
            scale = scale * (2.0 - pivot * scale)
            scale = scale * (2.0 - pivot * scale)
            for m in range(k + 1, 4):
                f = cols[m][o + k:o + k + 1, :] * scale
                rows[m] = rows[m] - f * rows[k]
                cols[m] = cols[m] - cols[k] * f
            work = work - jnp.where(rows_here > o + k, cols[k], 0.0) * (rows[k] * scale)
        if o == 4:
            done.append(work[:8])
            work = work[8:]
    full = jnp.concatenate(done, axis=0)
    diagonal = jnp.sum(jnp.where(lane == row, full, 0.0), axis=1, keepdims=True)
    return full * lax.rsqrt(diagonal)


def kernel(
    n, sections, tokens_all,
    x_hbm, gain_hbm, left_hbm, r_hbm, b_hbm,
    gain_out, bias_out, left_out, right_out,
    gain_ref, left_ref, x_v, rt, bt, scaled_v, bnd, acc1, acc2, wide, terms, terms_in, grams, ortho_v,
    sib_out, sib_in, cross_out, cross_in, shift_v,
    local_sem, r_recv, r_cross, r_sib, r_fwd, b_recv, b_cross, b_sib, b_fwd,
    t_send, t_recv, g_send, g_recv, o_send, o_recv,
    s_send, s_recv, c_send, c_recv, f_send, f_recv,
):
    me = lax.axis_index("dp")
    section = lax.axis_index("section")
    chips = n // 2
    chip, core = me // 2, me % 2
    sib = chip * 2 + (1 - core)
    tokens, d = x_v.shape
    w = d // n
    pw = w // IN_PIECES
    ow = w // OUT_PIECES

    loads = [
        pltpu.make_async_copy(r_hbm, rt.at[me], local_sem.at[0]),
        pltpu.make_async_copy(x_hbm, x_v, local_sem.at[1]),
        pltpu.make_async_copy(b_hbm, bt.at[me], local_sem.at[2]),
        pltpu.make_async_copy(gain_hbm, gain_ref, local_sem.at[3]),
        pltpu.make_async_copy(left_hbm, left_ref, local_sem.at[4]),
    ]
    for load in loads:
        load.start()

    barrier = pltpu.get_barrier_semaphore()
    for i in range(1, n):
        pl.semaphore_signal(barrier, inc=1, device_id={"dp": (me + i) % n}, device_id_type=pl.DeviceIdType.MESH)

    @pl.when(section < sections - 1)
    def _():
        pl.semaphore_signal(barrier, inc=1, device_id={"section": section + 1}, device_id_type=pl.DeviceIdType.MESH)

    pl.semaphore_wait(barrier, jnp.where(section > 0, n, n - 1))

    def piece(p):
        return pl.ds(pl.multiple_of(p * pw, LANES), pw)

    def columns(j, p):
        return pl.ds(pl.multiple_of(j * w + p * pw, LANES), pw)

    def other(o):
        return ((chip + o) % chips) * 2 + core

    def source(o):
        return ((chip + chips - o) % chips) * 2 + core

    def flip(j):
        return j + 1 - 2 * core

    def to_cross(src, buf, recv, send, o, p):
        return remote(src.at[:, piece(p)], buf.at[me, :, piece(p)], send.at[o, p], recv.at[me, p], dp=other(o))

    def to_sib(src, buf, recv, send, p):
        return remote(src.at[:, piece(p)], buf.at[me, :, piece(p)], send.at[p], recv.at[me, p], dp=sib)

    def forward(buf, recv, send, o, p):
        j = source(o)
        return remote(buf.at[j, :, piece(p)], buf.at[j, :, piece(p)], send.at[o, p], recv.at[j, p], dp=sib)

    def arrived(buf, recv, send, j, p):
        remote(buf.at[j, :, piece(p)], buf.at[j, :, piece(p)], send.at[0], recv.at[j, p], dp=sib).wait_recv()

    for p in range(IN_PIECES):
        for o in range(1, chips):
            to_cross(r_hbm, rt, r_recv, r_cross, o, p).start()
    for p in range(IN_PIECES):
        to_sib(r_hbm, rt, r_recv, r_sib, p).start()
    for p in range(IN_PIECES):
        for o in range(1, chips):
            to_cross(b_hbm, bt, b_recv, b_cross, o, p).start()

    step = d // 12
    loads[1].wait()

    def tiles(i):
        for c in range(step // LANES):
            yield x_v[:, pl.ds(pl.multiple_of(i * step + c * LANES, LANES), LANES)].astype(F32)

    def sum_step(i, acc):
        for tile in tiles(i):
            acc = acc + tile
        return acc

    zero = jnp.zeros((tokens, LANES), F32)
    mu = jnp.sum(lax.fori_loop(0, 12, sum_step, zero), axis=1, keepdims=True) / d
    mu_wide = jnp.broadcast_to(mu, (tokens, LANES))

    def square_step(i, acc):
        for tile in tiles(i):
            c = tile - mu_wide
            acc = acc + c * c
        return acc

    var = jnp.sum(lax.fori_loop(0, 12, square_step, zero), axis=1, keepdims=True) / d
    inverse = lax.rsqrt(var + 1e-5)

    loads[4].wait()
    left = left_ref[...].astype(F32).T.astype(BF16)
    acc1[...] = zero
    acc2[...] = zero
    wide[0] = mu_wide
    wide[1] = jnp.broadcast_to(inverse, (tokens, LANES))

    def first_pass(j, p):
        for c in range(pw // TILE):
            inside = pl.ds(pl.multiple_of(p * pw + c * TILE, LANES), TILE)
            rebuilt_tile = lax.dot_general(left, rt[j, :, inside], NN, preferred_element_type=F32)
            for l in range(TILE // LANES):
                offset = p * pw + c * TILE + l * LANES
                local = pl.ds(pl.multiple_of(offset, LANES), LANES)
                at = pl.ds(pl.multiple_of(j * w + offset, LANES), LANES)
                gain = jnp.broadcast_to(gain_ref[:, at], (8, LANES))[None]
                gain_sum = jnp.zeros((8, LANES), F32)
                bias_sum = jnp.zeros((8, LANES), F32)
                for h in range(0, tokens, ROWS):
                    rows = pl.ds(h, ROWS)
                    shape = (ROWS // 8, 8, LANES)
                    rebuilt = rebuilt_tile[h:h + ROWS, l * LANES:(l + 1) * LANES]
                    normed = (x_v[rows, at].astype(F32) - wide[0, rows, :]) * wide[1, rows, :]
                    product = (rebuilt * normed).reshape(shape)
                    rebuilt = rebuilt.reshape(shape)
                    gain_sum = gain_sum + jnp.sum(product, axis=0)
                    bias_sum = bias_sum + jnp.sum(rebuilt, axis=0)
                    scaled = (rebuilt * gain).reshape(ROWS, LANES)
                    scaled_v[rows, at] = scaled
                    acc1[rows, :] += scaled
                    acc2[rows, :] += (product * gain).reshape(ROWS, LANES)
                terms[j, 0:1, local] = jnp.sum(gain_sum, axis=0, keepdims=True)
                terms[j, 1:2, local] = jnp.sum(bias_sum, axis=0, keepdims=True)

    def loop(count, body):
        lax.fori_loop(0, count, lambda i, _: (body(i), 0)[1], 0)

    loads[0].wait()
    loads[3].wait()
    loop(IN_PIECES, lambda p: first_pass(me, p))

    def sib_first(p):
        arrived(rt, r_recv, r_sib, sib, p)
        first_pass(sib, p)

    loop(IN_PIECES, sib_first)

    def cross_first(i):
        p, o = i // (chips - 1), 1 + i % (chips - 1)
        arrived(rt, r_recv, r_sib, source(o), p)
        forward(rt, r_recv, r_fwd, o, p).start()
        first_pass(source(o), p)

    loop(IN_PIECES * (chips - 1), cross_first)
    loop(IN_PIECES, lambda p: to_sib(b_hbm, bt, b_recv, b_sib, p).start())

    def forwarded_first(i):
        p, o = i // (chips - 1), 1 + i % (chips - 1)
        arrived(rt, r_recv, r_sib, flip(source(o)), p)
        first_pass(flip(source(o)), p)

    loop(IN_PIECES * (chips - 1), forwarded_first)

    m1 = jnp.sum(acc1[...], axis=1, keepdims=True) / d * inverse
    m2 = jnp.sum(acc2[...], axis=1, keepdims=True) / d * inverse * inverse

    wide[0] = jnp.broadcast_to(m1 - mu * m2, (tokens, LANES))
    wide[2] = jnp.broadcast_to(m2, (tokens, LANES))

    def second_pass(j, p):
        for h in range(0, tokens, ROWS):
            rows = pl.ds(h, ROWS)
            shift, scale, slope = wide[0, rows, :], wide[1, rows, :], wide[2, rows, :]
            for l in range(pw // LANES):
                at = pl.ds(pl.multiple_of(j * w + p * pw + l * LANES, LANES), LANES)
                bnd[rows, at] = (scaled_v[rows, at] * scale - x_v[rows, at].astype(F32) * slope - shift).astype(BF16)

    def project(j, p):
        acc1[0:64, :] += lax.dot_general(bt[j, :, piece(p)], bnd[:, columns(j, p)], NT, preferred_element_type=F32)

    acc1[...] = zero
    loads[2].wait()

    def own_second(p):
        second_pass(me, p)
        project(me, p)

    loop(IN_PIECES, own_second)

    def sib_second(p):
        second_pass(sib, p)
        arrived(bt, b_recv, b_sib, sib, p)
        project(sib, p)

    loop(IN_PIECES, sib_second)

    def cross_second(i):
        p, o = i // (chips - 1), 1 + i % (chips - 1)
        second_pass(source(o), p)
        second_pass(flip(source(o)), p)
        arrived(bt, b_recv, b_sib, source(o), p)
        forward(bt, b_recv, b_fwd, o, p).start()
        project(source(o), p)

    loop(IN_PIECES * (chips - 1), cross_second)

    def forwarded_second(i):
        p, o = i // (chips - 1), 1 + i % (chips - 1)
        arrived(bt, b_recv, b_sib, flip(source(o)), p)
        project(flip(source(o)), p)

    loop(IN_PIECES * (chips - 1), forwarded_second)

    r = left_ref.shape[0]
    power = acc1[0:64, :]
    half = r // 2
    tall = jnp.concatenate([power, jnp.zeros_like(power)], axis=0)
    low = jnp.concatenate([jnp.zeros_like(power), power], axis=0)
    grams[me] = lax.dot_general(
        power[0:half], tall, NT, precision=HIGH, preferred_element_type=F32
    ) + lax.dot_general(power[half:r], low, NT, precision=HIGH, preferred_element_type=F32)

    def gram_copy(i):
        return remote(grams.at[me], grams.at[me], g_send.at[i], g_recv.at[me], dp=(me + i) % n)

    def terms_copy(i):
        to = (me + i) % n
        return remote(terms.at[to], terms_in.at[me], t_send.at[i], t_recv.at[me], dp=to)

    for i in range(1, n):
        gram_copy(i).start()
    for i in range(1, n):
        j = (me + i) % n
        remote(grams.at[j], grams.at[j], g_send.at[0], g_recv.at[j], dp=sib).wait_recv()
    for i in range(1, n):
        terms_copy(i).start()
    packed = grams[0]
    for j in range(1, n):
        packed = packed + grams[j]
    factor = inverse_factor(jnp.concatenate([packed, pltpu.roll(packed, r, 1)], axis=0))
    ortho = lax.dot_general(factor, low, NN, precision=HIGH, preferred_element_type=F32).astype(BF16)
    ortho_v[...] = ortho

    def ortho_copy():
        return remote(ortho_v, left_out, o_send, o_recv, section=section - 1)

    @pl.when(section > 0)
    def _():
        ortho_copy().start()

    def out_piece(q):
        return pl.ds(pl.multiple_of(q * ow, LANES), ow)

    def share(j, q):
        at = pl.ds(pl.multiple_of(j * w + q * ow, LANES), ow)
        return lax.dot_general(ortho_v[...], bnd[:, at], NN, preferred_element_type=F32)

    def sib_copy(o, q):
        return remote(sib_out.at[o, :, out_piece(q)], sib_in.at[o, :, out_piece(q)], s_send.at[o, q], s_recv.at[o, q], dp=sib)

    def cross_copy(o, q):
        return remote(cross_out.at[o, :, out_piece(q)], cross_in.at[o, :, out_piece(q)], c_send.at[o, q], c_recv.at[o, q], dp=other(o))

    def shift_copy(q):
        return remote(shift_v.at[:, out_piece(q)], right_out.at[:, out_piece(q)], f_send.at[q], f_recv.at[q], section=section - 1)

    def send_sib(o, q):
        sib_out[o, :, out_piece(q)] = share(flip(other(o)), q).astype(BF16)
        sib_copy(o, q).start()

    def split(i):
        return 1 + i % (chips - 1), i // (chips - 1)

    def stage_a(i):
        o, q = split(i)
        send_sib(o, q)

    loop(OUT_PIECES * (chips - 1), stage_a)

    def stage_b(i):
        o, q = split(i)
        mine = share(other(o), q)
        sib_copy(o, q).wait_recv()
        cross_out[o, :, out_piece(q)] = (mine + sib_in[o, :, out_piece(q)].astype(F32)).astype(BF16)
        cross_copy(o, q).start()

    loop(OUT_PIECES * (chips - 1), stage_b)
    loop(OUT_PIECES, lambda q: send_sib(0, q))

    for i in range(1, n):
        j = (me + i) % n
        remote(terms.at[j], terms_in.at[j], t_send.at[0], t_recv.at[j], dp=sib).wait_recv()
    sums = terms[me]
    for i in range(1, n):
        sums = sums + terms_in[(me + i) % n]
    sums = sums * (1.0 / tokens_all ** 0.5)
    gain_out[...] = sums[0:1]
    bias_out[...] = sums[1:2]

    def stage_c(q):
        total = share(me, q)
        sib_copy(0, q).wait_recv()
        total = total + sib_in[0, :, out_piece(q)].astype(F32)
        for o in range(1, chips):
            cross_copy(o, q).wait_recv()
            total = total + cross_in[o, :, out_piece(q)].astype(F32)
        shift_v[:, out_piece(q)] = total.astype(BF16)

        @pl.when(section > 0)
        def _():
            shift_copy(q).start()

    loop(OUT_PIECES, stage_c)

    @pl.when(section == sections - 1)
    def _():
        left_out[...] = jnp.zeros_like(left_out)
        right_out[...] = jnp.zeros_like(right_out)

    def inputs_sent(i):
        p, o = i // (chips - 1), 1 + i % (chips - 1)
        to_cross(r_hbm, rt, r_recv, r_cross, o, p).wait_send()
        to_cross(b_hbm, bt, b_recv, b_cross, o, p).wait_send()
        forward(rt, r_recv, r_fwd, o, p).wait_send()
        forward(bt, b_recv, b_fwd, o, p).wait_send()

    loop(IN_PIECES * (chips - 1), inputs_sent)

    def inputs_sent_sib(p):
        to_sib(r_hbm, rt, r_recv, r_sib, p).wait_send()
        to_sib(b_hbm, bt, b_recv, b_sib, p).wait_send()

    loop(IN_PIECES, inputs_sent_sib)
    for i in range(1, n):
        gram_copy(i).wait_send()
        terms_copy(i).wait_send()

    def shares_sent(i):
        o, q = split(i)
        sib_copy(o, q).wait_send()
        cross_copy(o, q).wait_send()

    loop(OUT_PIECES * (chips - 1), shares_sent)
    loop(OUT_PIECES, lambda q: sib_copy(0, q).wait_send())

    @pl.when(section < sections - 1)
    def _():
        ortho_copy().wait_recv()
        loop(OUT_PIECES, lambda q: shift_copy(q).wait_recv())

    @pl.when(section > 0)
    def _():
        ortho_copy().wait_send()
        loop(OUT_PIECES, lambda q: shift_copy(q).wait_send())


def write_out(*refs):
    come = [pltpu.make_async_copy(refs[i], refs[8 + i], refs[12].at[i]) for i in range(4)]
    go = [pltpu.make_async_copy(refs[8 + i], refs[4 + i], refs[13].at[i]) for i in range(4)]
    for copy in come:
        copy.start()
    for first, second in zip(come, go):
        first.wait()
        second.start()
    for copy in go:
        copy.wait()


def on_device(n, sections, saved_input, norm_gain, left_in, right_in, basis):
    _, tokens, d = saved_input.shape
    r = left_in.shape[2]
    w = d // n
    chips = n // 2
    vmem = pl.BlockSpec(memory_space=pltpu.VMEM)
    hbm = pl.BlockSpec(memory_space=pltpu.HBM)
    dma = pltpu.SemaphoreType.DMA
    gather = [dma((n, IN_PIECES)), dma((chips, IN_PIECES)), dma((IN_PIECES,)), dma((chips, IN_PIECES))]
    results = (
        jax.ShapeDtypeStruct((1, w), F32),
        jax.ShapeDtypeStruct((1, w), F32),
        jax.ShapeDtypeStruct((r, tokens), BF16),
        jax.ShapeDtypeStruct((r, w), BF16),
    )
    held = pl.pallas_call(
        functools.partial(kernel, n, sections, tokens * n),
        out_shape=results,
        in_specs=[hbm] * 5,
        out_specs=(vmem, vmem, vmem, vmem),
        scratch_shapes=[
            pltpu.VMEM((1, d), F32),
            pltpu.VMEM((r, tokens), BF16),
            pltpu.VMEM((tokens, d), BF16),
            pltpu.VMEM((n, r, w), BF16),
            pltpu.VMEM((n, r, w), BF16),
            pltpu.VMEM((tokens, d), F32),
            pltpu.VMEM((tokens, d), BF16),
            pltpu.VMEM((tokens, LANES), F32),
            pltpu.VMEM((tokens, LANES), F32),
            pltpu.VMEM((3, tokens, LANES), F32),
            pltpu.VMEM((n, 2, w), F32),
            pltpu.VMEM((n, 2, w), F32),
            pltpu.VMEM((n, r // 2, 2 * r), F32),
            pltpu.VMEM((r, tokens), BF16),
            pltpu.VMEM((chips, r, w), BF16),
            pltpu.VMEM((chips, r, w), BF16),
            pltpu.VMEM((chips, r, w), BF16),
            pltpu.VMEM((chips, r, w), BF16),
            pltpu.VMEM((r, w), BF16),
            dma((5,)),
            *gather,
            *gather,
            dma((n,)), dma((n,)),
            dma((n,)), dma((n,)),
            dma, dma,
            dma((chips, OUT_PIECES)), dma((chips, OUT_PIECES)),
            dma((chips, OUT_PIECES)), dma((chips, OUT_PIECES)),
            dma((OUT_PIECES,)), dma((OUT_PIECES,)),
        ],
        compiler_params=pltpu.CompilerParams(
            collective_id=0, has_side_effects=True, vmem_limit_bytes=63 * 1024 * 1024
        ),
    )(saved_input[0], norm_gain, left_in[0].T, right_in[0].T, basis[0].T)
    gain, bias, left, right = pl.pallas_call(
        write_out,
        out_shape=results,
        in_specs=[hbm] * 4,
        out_specs=(hbm,) * 4,
        scratch_shapes=[*(pltpu.VMEM(a.shape, a.dtype) for a in results), dma((4,)), dma((4,))],
        compiler_params=pltpu.CompilerParams(vmem_limit_bytes=63 * 1024 * 1024),
    )(*held)
    return gain, bias, left.T[None], right.T[None]


def solution(mesh):
    placed = (
        P("section", "dp", None),
        P("section", None),
        P("section", "dp", None),
        P("section", "dp", None),
        P("section", "dp", None),
    )
    return jax.shard_map(
        functools.partial(on_device, mesh.shape["dp"], mesh.shape["section"]),
        mesh=mesh,
        in_specs=placed,
        out_specs=(
            P("section", "dp"),
            P("section", "dp"),
            P("section", "dp", None),
            P("section", "dp", None),
        ),
        check_vma=False,
    )
```

```python
import functools

import jax
import jax.numpy as jnp
from jax import lax
from jax.experimental import pallas as pl
from jax.experimental.pallas import tpu as pltpu
from jax.sharding import PartitionSpec as P

F32 = jnp.float32
BF16 = jnp.bfloat16
HIGH = lax.Precision.HIGHEST
NN = (((1,), (0,)), ((), ()))
NT = (((1,), (1,)), ((), ()))
LANES = 128
IN_PIECES = 3
OUT_PIECES = 6
TILE = 256
ROWS = 32


def remote(src, dst, send, recv, **where):
    return pltpu.make_async_remote_copy(
        src_ref=src, dst_ref=dst, send_sem=send, recv_sem=recv,
        device_id=where, device_id_type=pl.DeviceIdType.MESH,
    )


def inverse_factor(gram):
    r, width = gram.shape
    row = lax.broadcasted_iota(jnp.int32, (r, width), 0)
    lane = lax.broadcasted_iota(jnp.int32, (r, width), 1)
    work = jnp.where(lane < r, gram, jnp.where(lane == row + r, 1.0, 0.0))
    done = []
    for j0 in range(0, r, 4):
        base = (j0 // 8) * 8
        o = j0 - base
        rows_here = lax.broadcasted_iota(jnp.int32, work.shape, 0)
        cols = [jnp.broadcast_to(work[:, j0 + k:j0 + k + 1], work.shape) for k in range(4)]
        rows = [work[o + k:o + k + 1, :] for k in range(4)]
        for k in range(4):
            pivot = cols[k][o + k:o + k + 1, :]
            scale = pl.reciprocal(pivot, approx=True)
            scale = scale * (2.0 - pivot * scale)
            scale = scale * (2.0 - pivot * scale)
            for m in range(k + 1, 4):
                f = cols[m][o + k:o + k + 1, :] * scale
                rows[m] = rows[m] - f * rows[k]
                cols[m] = cols[m] - cols[k] * f
            work = work - jnp.where(rows_here > o + k, cols[k], 0.0) * (rows[k] * scale)
        if o == 4:
            done.append(work[:8])
            work = work[8:]
    full = jnp.concatenate(done, axis=0)
    diagonal = jnp.sum(jnp.where(lane == row, full, 0.0), axis=1, keepdims=True)
    return full * lax.rsqrt(diagonal)


def kernel(
    n, sections, tokens_all,
    x_hbm, gain_hbm, left_hbm, r_hbm, b_hbm,
    gain_out, bias_out, left_out, right_out,
    gain_ref, left_ref, x_v, rt, bt, scaled_v, bnd, acc1, acc2, wide, terms, terms_in, grams, ortho_v, power_v, pre, conditioner,
    sib_out, sib_in, cross_out, cross_in, shift_v,
    local_sem, r_recv, r_cross, r_sib, r_fwd, b_recv, b_cross, b_sib, b_fwd,
    p_send, p_recv, t_send, t_recv, g_send, g_recv, o_send, o_recv,
    s_send, s_recv, c_send, c_recv, f_send, f_recv,
):
    me = lax.axis_index("dp")
    section = lax.axis_index("section")
    chips = n // 2
    chip, core = me // 2, me % 2
    sib = chip * 2 + (1 - core)
    tokens, d = x_v.shape
    w = d // n
    pw = w // IN_PIECES
    ow = w // OUT_PIECES

    loads = [
        pltpu.make_async_copy(r_hbm, rt.at[me], local_sem.at[0]),
        pltpu.make_async_copy(x_hbm, x_v, local_sem.at[1]),
        pltpu.make_async_copy(b_hbm, bt.at[me], local_sem.at[2]),
        pltpu.make_async_copy(gain_hbm, gain_ref, local_sem.at[3]),
        pltpu.make_async_copy(left_hbm, left_ref, local_sem.at[4]),
    ]
    for load in loads:
        load.start()

    barrier = pltpu.get_barrier_semaphore()
    for i in range(1, n):
        pl.semaphore_signal(barrier, inc=1, device_id={"dp": (me + i) % n}, device_id_type=pl.DeviceIdType.MESH)

    @pl.when(section < sections - 1)
    def _():
        pl.semaphore_signal(barrier, inc=1, device_id={"section": section + 1}, device_id_type=pl.DeviceIdType.MESH)

    pl.semaphore_wait(barrier, jnp.where(section > 0, n, n - 1))

    def piece(p):
        return pl.ds(pl.multiple_of(p * pw, LANES), pw)

    def columns(j, p):
        return pl.ds(pl.multiple_of(j * w + p * pw, LANES), pw)

    def other(o):
        return ((chip + o) % chips) * 2 + core

    def source(o):
        return ((chip + chips - o) % chips) * 2 + core

    def flip(j):
        return j + 1 - 2 * core

    def to_cross(src, buf, recv, send, o, p):
        return remote(src.at[:, piece(p)], buf.at[me, :, piece(p)], send.at[o, p], recv.at[me, p], dp=other(o))

    def to_sib(src, buf, recv, send, p):
        return remote(src.at[:, piece(p)], buf.at[me, :, piece(p)], send.at[p], recv.at[me, p], dp=sib)

    def forward(buf, recv, send, o, p):
        j = source(o)
        return remote(buf.at[j, :, piece(p)], buf.at[j, :, piece(p)], send.at[o, p], recv.at[j, p], dp=sib)

    def arrived(buf, recv, send, j, p):
        remote(buf.at[j, :, piece(p)], buf.at[j, :, piece(p)], send.at[0], recv.at[j, p], dp=sib).wait_recv()

    for p in range(IN_PIECES):
        for o in range(1, chips):
            to_cross(r_hbm, rt, r_recv, r_cross, o, p).start()
    for p in range(IN_PIECES):
        to_sib(r_hbm, rt, r_recv, r_sib, p).start()
    step = d // 12
    loads[1].wait()

    def tiles(i):
        for c in range(step // LANES):
            yield x_v[:, pl.ds(pl.multiple_of(i * step + c * LANES, LANES), LANES)].astype(F32)

    def sum_step(i, acc):
        for tile in tiles(i):
            acc = acc + tile
        return acc

    zero = jnp.zeros((tokens, LANES), F32)
    mu = jnp.sum(lax.fori_loop(0, 12, sum_step, zero), axis=1, keepdims=True) / d
    mu_wide = jnp.broadcast_to(mu, (tokens, LANES))

    def square_step(i, acc):
        for tile in tiles(i):
            c = tile - mu_wide
            acc = acc + c * c
        return acc

    var = jnp.sum(lax.fori_loop(0, 12, square_step, zero), axis=1, keepdims=True) / d
    inverse = lax.rsqrt(var + 1e-5)

    loads[4].wait()
    left = left_ref[...].astype(F32).T.astype(BF16)
    acc1[...] = zero
    acc2[...] = zero
    wide[0] = mu_wide
    wide[1] = jnp.broadcast_to(inverse, (tokens, LANES))

    loads[0].wait()
    loads[2].wait()
    loads[3].wait()
    r = left_ref.shape[0]

    def stack(top, bottom):
        return jnp.concatenate([top, bottom], axis=0)

    def moments(p, carry):
        product, sums = carry
        scaled = rt[me, :, piece(p)].astype(F32) * gain_ref[:, columns(me, p)]
        high = scaled.astype(BF16)
        low = (scaled - high.astype(F32)).astype(BF16)
        both = bt[me, :, piece(p)]
        nothing = jnp.zeros_like(both)
        ones = jnp.ones((16, pw), BF16)
        right = stack(both, nothing)
        for part in (high, low):
            product = product + lax.dot_general(part, right, NT, preferred_element_type=F32)
            sums = sums + lax.dot_general(ones, stack(nothing, part), NT, preferred_element_type=F32)
        return product, sums + lax.dot_general(ones, right, NT, preferred_element_type=F32)

    product, sums = lax.fori_loop(0, IN_PIECES, moments, (jnp.zeros((r, 2 * r), F32), jnp.zeros((16, 2 * r), F32)))
    weighted = (left.astype(F32) * inverse).T
    spread = lax.dot_general(weighted, stack(jnp.zeros_like(weighted), weighted), NT, precision=HIGH, preferred_element_type=F32)
    pre[me, 0:r, :] = product + spread
    pre[me, r:r + 8, :] = sums[0:8]

    def pre_copy(i):
        return remote(pre.at[me], pre.at[me], p_send.at[i], p_recv.at[me], dp=(me + i) % n)

    for i in range(1, n):
        pre_copy(i).start()

    for p in range(IN_PIECES):
        for o in range(1, chips):
            to_cross(b_hbm, bt, b_recv, b_cross, o, p).start()

    def first_pass(j, p):
        for c in range(pw // TILE):
            inside = pl.ds(pl.multiple_of(p * pw + c * TILE, LANES), TILE)
            rebuilt_tile = lax.dot_general(left, rt[j, :, inside], NN, preferred_element_type=F32)
            for l in range(TILE // LANES):
                offset = p * pw + c * TILE + l * LANES
                local = pl.ds(pl.multiple_of(offset, LANES), LANES)
                at = pl.ds(pl.multiple_of(j * w + offset, LANES), LANES)
                gain = jnp.broadcast_to(gain_ref[:, at], (8, LANES))[None]
                gain_sum = jnp.zeros((8, LANES), F32)
                bias_sum = jnp.zeros((8, LANES), F32)
                for h in range(0, tokens, ROWS):
                    rows = pl.ds(h, ROWS)
                    shape = (ROWS // 8, 8, LANES)
                    rebuilt = rebuilt_tile[h:h + ROWS, l * LANES:(l + 1) * LANES]
                    normed = (x_v[rows, at].astype(F32) - wide[0, rows, :]) * wide[1, rows, :]
                    product = (rebuilt * normed).reshape(shape)
                    rebuilt = rebuilt.reshape(shape)
                    gain_sum = gain_sum + jnp.sum(product, axis=0)
                    bias_sum = bias_sum + jnp.sum(rebuilt, axis=0)
                    scaled = (rebuilt * gain).reshape(ROWS, LANES)
                    scaled_v[rows, at] = scaled
                    acc1[rows, :] += scaled
                    acc2[rows, :] += (product * gain).reshape(ROWS, LANES)
                terms[j, 0:1, local] = jnp.sum(gain_sum, axis=0, keepdims=True)
                terms[j, 1:2, local] = jnp.sum(bias_sum, axis=0, keepdims=True)

    def loop(count, body):
        lax.fori_loop(0, count, lambda i, _: (body(i), 0)[1], 0)

    loop(IN_PIECES, lambda p: first_pass(me, p))

    def sib_first(p):
        arrived(rt, r_recv, r_sib, sib, p)
        first_pass(sib, p)

    loop(IN_PIECES, sib_first)

    def cross_first(i):
        p, o = i // (chips - 1), 1 + i % (chips - 1)
        arrived(rt, r_recv, r_sib, source(o), p)
        forward(rt, r_recv, r_fwd, o, p).start()
        first_pass(source(o), p)

    loop(IN_PIECES * (chips - 1), cross_first)
    loop(IN_PIECES, lambda p: to_sib(b_hbm, bt, b_recv, b_sib, p).start())

    for i in range(1, n):
        j = (me + i) % n
        remote(pre.at[j], pre.at[j], p_send.at[0], p_recv.at[j], dp=sib).wait_recv()
    whole = pre[0]
    for j in range(1, n):
        whole = whole + pre[j]
    tile, sums = whole[0:r], whole[r:r + 8]
    row = lax.broadcasted_iota(jnp.int32, (r, 2 * r), 0)
    lane = lax.broadcasted_iota(jnp.int32, (r, 2 * r), 1)
    pick = jnp.where(lane == row + r, 1.0, 0.0)
    r_sums = lax.dot_general(pick, sums, NT, precision=HIGH, preferred_element_type=F32)
    b_sums = jnp.where(lane[0:8] < r, sums, 0.0) * (1.0 / (8 * d))
    moment = jnp.where(lane < r, tile, 0.0) - lax.dot_general(r_sums, b_sums, NN, precision=HIGH, preferred_element_type=F32)
    moved = lax.dot_general(tile[:, r:], moment, NN, precision=HIGH, preferred_element_type=F32)
    turned = moment.T[0:r]
    guess = lax.dot_general(turned, moved, NN, precision=HIGH, preferred_element_type=F32)
    diagonal = jnp.where(lane == row, guess, 0.0)
    level = jnp.sum(jnp.sum(diagonal, axis=1, keepdims=True), axis=0, keepdims=True) * (1e-4 / r) + 1e-30
    conditioner[...] = inverse_factor(guess + jnp.where(lane == row, level, 0.0))

    def forwarded_first(i):
        p, o = i // (chips - 1), 1 + i % (chips - 1)
        arrived(rt, r_recv, r_sib, flip(source(o)), p)
        first_pass(flip(source(o)), p)

    loop(IN_PIECES * (chips - 1), forwarded_first)

    m1 = jnp.sum(acc1[...], axis=1, keepdims=True) / d * inverse
    m2 = jnp.sum(acc2[...], axis=1, keepdims=True) / d * inverse * inverse

    wide[0] = jnp.broadcast_to(m1 - mu * m2, (tokens, LANES))
    wide[2] = jnp.broadcast_to(m2, (tokens, LANES))

    def second_pass(j, p):
        for h in range(0, tokens, ROWS):
            rows = pl.ds(h, ROWS)
            shift, scale, slope = wide[0, rows, :], wide[1, rows, :], wide[2, rows, :]
            for l in range(pw // LANES):
                at = pl.ds(pl.multiple_of(j * w + p * pw + l * LANES, LANES), LANES)
                bnd[rows, at] = (scaled_v[rows, at] * scale - x_v[rows, at].astype(F32) * slope - shift).astype(BF16)

    def project(j, p):
        acc1[0:r, :] += lax.dot_general(bt[j, :, piece(p)], bnd[:, columns(j, p)], NT, preferred_element_type=F32)

    acc1[...] = zero

    def own_second(p):
        second_pass(me, p)
        project(me, p)

    loop(IN_PIECES, own_second)

    def sib_second(p):
        second_pass(sib, p)
        arrived(bt, b_recv, b_sib, sib, p)
        project(sib, p)

    loop(IN_PIECES, sib_second)

    def cross_second(i):
        p, o = i // (chips - 1), 1 + i % (chips - 1)
        second_pass(source(o), p)
        second_pass(flip(source(o)), p)
        arrived(bt, b_recv, b_sib, source(o), p)
        forward(bt, b_recv, b_fwd, o, p).start()
        project(source(o), p)

    loop(IN_PIECES * (chips - 1), cross_second)

    def forwarded_second(i):
        p, o = i // (chips - 1), 1 + i % (chips - 1)
        arrived(bt, b_recv, b_sib, flip(source(o)), p)
        project(flip(source(o)), p)

    loop(IN_PIECES * (chips - 1), forwarded_second)

    plain = acc1[0:r, :]
    power = lax.dot_general(conditioner[...], stack(jnp.zeros_like(plain), plain), NN, precision=HIGH, preferred_element_type=F32)
    power_v[...] = power.astype(BF16)

    def out_piece(q):
        return pl.ds(pl.multiple_of(q * ow, LANES), ow)

    def share(j, q):
        at = pl.ds(pl.multiple_of(j * w + q * ow, LANES), ow)
        return lax.dot_general(power_v[...], bnd[:, at], NN, preferred_element_type=F32)

    def sib_copy(o, q):
        return remote(sib_out.at[o, :, out_piece(q)], sib_in.at[o, :, out_piece(q)], s_send.at[o, q], s_recv.at[o, q], dp=sib)

    def cross_copy(o, q):
        return remote(cross_out.at[o, :, out_piece(q)], cross_in.at[o, :, out_piece(q)], c_send.at[o, q], c_recv.at[o, q], dp=other(o))

    def shift_copy(q):
        return remote(shift_v.at[:, out_piece(q)], right_out.at[:, out_piece(q)], f_send.at[q], f_recv.at[q], section=section - 1)

    def send_sib(o, q):
        sib_out[o, :, out_piece(q)] = share(flip(other(o)), q).astype(BF16)
        sib_copy(o, q).start()

    def split(i):
        return 1 + i % (chips - 1), i // (chips - 1)

    def stage_a(i):
        o, q = split(i)
        send_sib(o, q)

    loop(OUT_PIECES * (chips - 1), stage_a)

    half = r // 2
    nothing = jnp.zeros_like(power)
    grams[me] = lax.dot_general(
        power[0:half], stack(power, nothing), NT, precision=HIGH, preferred_element_type=F32
    ) + lax.dot_general(power[half:r], stack(nothing, power), NT, precision=HIGH, preferred_element_type=F32)

    def gram_copy(i):
        return remote(grams.at[me], grams.at[me], g_send.at[i], g_recv.at[me], dp=(me + i) % n)

    def terms_copy(i):
        to = (me + i) % n
        return remote(terms.at[to], terms_in.at[me], t_send.at[i], t_recv.at[me], dp=to)

    for i in range(1, n):
        gram_copy(i).start()


    def stage_b(i):
        o, q = split(i)
        mine = share(other(o), q)
        sib_copy(o, q).wait_recv()
        cross_out[o, :, out_piece(q)] = (mine + sib_in[o, :, out_piece(q)].astype(F32)).astype(BF16)
        cross_copy(o, q).start()

    loop(OUT_PIECES * (chips - 1), stage_b)
    loop(OUT_PIECES, lambda q: send_sib(0, q))

    for i in range(1, n):
        terms_copy(i).start()
    for i in range(1, n):
        j = (me + i) % n
        remote(grams.at[j], grams.at[j], g_send.at[0], g_recv.at[j], dp=sib).wait_recv()
    packed = grams[0]
    for j in range(1, n):
        packed = packed + grams[j]
    factor = inverse_factor(stack(packed, pltpu.roll(packed, r, 1)))
    conditioner[...] = factor
    ortho_v[...] = lax.dot_general(factor, stack(nothing, power), NN, precision=HIGH, preferred_element_type=F32).astype(BF16)

    def ortho_copy():
        return remote(ortho_v, left_out, o_send, o_recv, section=section - 1)

    @pl.when(section > 0)
    def _():
        ortho_copy().start()

    for i in range(1, n):
        j = (me + i) % n
        remote(terms.at[j], terms_in.at[j], t_send.at[0], t_recv.at[j], dp=sib).wait_recv()
    sums = terms[me]
    for i in range(1, n):
        sums = sums + terms_in[(me + i) % n]
    sums = sums * (1.0 / tokens_all ** 0.5)
    gain_out[...] = sums[0:1]
    bias_out[...] = sums[1:2]

    def stage_c(q):
        total = share(me, q)
        sib_copy(0, q).wait_recv()
        total = total + sib_in[0, :, out_piece(q)].astype(F32)
        for o in range(1, chips):
            cross_copy(o, q).wait_recv()
            total = total + cross_in[o, :, out_piece(q)].astype(F32)
        total = lax.dot_general(conditioner[...], stack(jnp.zeros_like(total), total), NN, precision=HIGH, preferred_element_type=F32)
        shift_v[:, out_piece(q)] = total.astype(BF16)

        @pl.when(section > 0)
        def _():
            shift_copy(q).start()

    loop(OUT_PIECES, stage_c)

    @pl.when(section == sections - 1)
    def _():
        left_out[...] = jnp.zeros_like(left_out)
        right_out[...] = jnp.zeros_like(right_out)

    def inputs_sent(i):
        p, o = i // (chips - 1), 1 + i % (chips - 1)
        to_cross(r_hbm, rt, r_recv, r_cross, o, p).wait_send()
        to_cross(b_hbm, bt, b_recv, b_cross, o, p).wait_send()
        forward(rt, r_recv, r_fwd, o, p).wait_send()
        forward(bt, b_recv, b_fwd, o, p).wait_send()

    loop(IN_PIECES * (chips - 1), inputs_sent)

    def inputs_sent_sib(p):
        to_sib(r_hbm, rt, r_recv, r_sib, p).wait_send()
        to_sib(b_hbm, bt, b_recv, b_sib, p).wait_send()

    loop(IN_PIECES, inputs_sent_sib)
    for i in range(1, n):
        gram_copy(i).wait_send()
        terms_copy(i).wait_send()
        pre_copy(i).wait_send()

    def shares_sent(i):
        o, q = split(i)
        sib_copy(o, q).wait_send()
        cross_copy(o, q).wait_send()

    loop(OUT_PIECES * (chips - 1), shares_sent)
    loop(OUT_PIECES, lambda q: sib_copy(0, q).wait_send())

    @pl.when(section < sections - 1)
    def _():
        ortho_copy().wait_recv()
        loop(OUT_PIECES, lambda q: shift_copy(q).wait_recv())

    @pl.when(section > 0)
    def _():
        ortho_copy().wait_send()
        loop(OUT_PIECES, lambda q: shift_copy(q).wait_send())


def write_out(*refs):
    come = [pltpu.make_async_copy(refs[i], refs[8 + i], refs[12].at[i]) for i in range(4)]
    go = [pltpu.make_async_copy(refs[8 + i], refs[4 + i], refs[13].at[i]) for i in range(4)]
    for copy in come:
        copy.start()
    for first, second in zip(come, go):
        first.wait()
        second.start()
    for copy in go:
        copy.wait()


def on_device(n, sections, saved_input, norm_gain, left_in, right_in, basis):
    _, tokens, d = saved_input.shape
    r = left_in.shape[2]
    w = d // n
    chips = n // 2
    vmem = pl.BlockSpec(memory_space=pltpu.VMEM)
    hbm = pl.BlockSpec(memory_space=pltpu.HBM)
    dma = pltpu.SemaphoreType.DMA
    gather = [dma((n, IN_PIECES)), dma((chips, IN_PIECES)), dma((IN_PIECES,)), dma((chips, IN_PIECES))]
    results = (
        jax.ShapeDtypeStruct((1, w), F32),
        jax.ShapeDtypeStruct((1, w), F32),
        jax.ShapeDtypeStruct((r, tokens), BF16),
        jax.ShapeDtypeStruct((r, w), BF16),
    )
    held = pl.pallas_call(
        functools.partial(kernel, n, sections, tokens * n),
        out_shape=results,
        in_specs=[hbm] * 5,
        out_specs=(vmem, vmem, vmem, vmem),
        scratch_shapes=[
            pltpu.VMEM((1, d), F32),
            pltpu.VMEM((r, tokens), BF16),
            pltpu.VMEM((tokens, d), BF16),
            pltpu.VMEM((n, r, w), BF16),
            pltpu.VMEM((n, r, w), BF16),
            pltpu.VMEM((tokens, d), F32),
            pltpu.VMEM((tokens, d), BF16),
            pltpu.VMEM((tokens, LANES), F32),
            pltpu.VMEM((tokens, LANES), F32),
            pltpu.VMEM((3, tokens, LANES), F32),
            pltpu.VMEM((n, 2, w), F32),
            pltpu.VMEM((n, 2, w), F32),
            pltpu.VMEM((n, r // 2, 2 * r), F32),
            pltpu.VMEM((r, tokens), BF16),
            pltpu.VMEM((r, tokens), BF16),
            pltpu.VMEM((n, r + 8, 2 * r), F32),
            pltpu.VMEM((r, 2 * r), F32),
            pltpu.VMEM((chips, r, w), BF16),
            pltpu.VMEM((chips, r, w), BF16),
            pltpu.VMEM((chips, r, w), BF16),
            pltpu.VMEM((chips, r, w), BF16),
            pltpu.VMEM((r, w), BF16),
            dma((5,)),
            *gather,
            *gather,
            dma((n,)), dma((n,)),
            dma((n,)), dma((n,)),
            dma((n,)), dma((n,)),
            dma, dma,
            dma((chips, OUT_PIECES)), dma((chips, OUT_PIECES)),
            dma((chips, OUT_PIECES)), dma((chips, OUT_PIECES)),
            dma((OUT_PIECES,)), dma((OUT_PIECES,)),
        ],
        compiler_params=pltpu.CompilerParams(
            collective_id=0, has_side_effects=True, vmem_limit_bytes=63 * 1024 * 1024
        ),
    )(saved_input[0], norm_gain, left_in[0].T, right_in[0].T, basis[0].T)
    gain, bias, left, right = pl.pallas_call(
        write_out,
        out_shape=results,
        in_specs=[hbm] * 4,
        out_specs=(hbm,) * 4,
        scratch_shapes=[*(pltpu.VMEM(a.shape, a.dtype) for a in results), dma((4,)), dma((4,))],
        compiler_params=pltpu.CompilerParams(vmem_limit_bytes=63 * 1024 * 1024),
    )(*held)
    return gain, bias, left.T[None], right.T[None]


def solution(mesh):
    placed = (
        P("section", "dp", None),
        P("section", None),
        P("section", "dp", None),
        P("section", "dp", None),
        P("section", "dp", None),
    )
    return jax.shard_map(
        functools.partial(on_device, mesh.shape["dp"], mesh.shape["section"]),
        mesh=mesh,
        in_specs=placed,
        out_specs=(
            P("section", "dp"),
            P("section", "dp"),
            P("section", "dp", None),
            P("section", "dp", None),
        ),
        check_vma=False,
    )
```

```python
import functools

import jax
import jax.numpy as jnp
from jax import lax
from jax.experimental import pallas as pl
from jax.experimental.pallas import tpu as pltpu
from jax.sharding import PartitionSpec as P

F32 = jnp.float32
BF16 = jnp.bfloat16
HIGH = lax.Precision.HIGHEST
NN = (((1,), (0,)), ((), ()))
NT = (((1,), (1,)), ((), ()))
LANES = 128
IN_PIECES = 3
OUT_PIECES = 6
TILE = 256
ROWS = 32


def remote(src, dst, send, recv, **where):
    return pltpu.make_async_remote_copy(
        src_ref=src, dst_ref=dst, send_sem=send, recv_sem=recv,
        device_id=where, device_id_type=pl.DeviceIdType.MESH,
    )


def inverse_factor(gram):
    r, width = gram.shape
    row = lax.broadcasted_iota(jnp.int32, (r, width), 0)
    lane = lax.broadcasted_iota(jnp.int32, (r, width), 1)
    work = jnp.where(lane < r, gram, jnp.where(lane == row + r, 1.0, 0.0))
    done = []
    for j0 in range(0, r, 8):
        cols = [jnp.broadcast_to(work[:, j0 + k:j0 + k + 1], work.shape) for k in range(8)]
        rows = [work[k:k + 1, :] for k in range(8)]
        work = work[8:]
        for k in range(8):
            pivot = cols[k][k:k + 1, :]
            scale = pl.reciprocal(pivot, approx=True)
            scale = scale * (2.0 - pivot * scale)
            scale = scale * (2.0 - pivot * scale)
            for m in range(k + 1, 8):
                f = cols[m][k:k + 1, :] * scale
                rows[m] = rows[m] - f * rows[k]
                cols[m] = cols[m] - cols[k] * f
            if j0 + 8 < r:
                work = work - cols[k][8:] * (rows[k] * scale)
        done.append(jnp.concatenate(rows, axis=0))
    full = jnp.concatenate(done, axis=0)
    diagonal = jnp.sum(jnp.where(lane == row, full, 0.0), axis=1, keepdims=True)
    return full * lax.rsqrt(diagonal)


def kernel(
    n, sections, tokens_all,
    x_hbm, gain_hbm, left_hbm, r_hbm, b_hbm,
    gain_out, bias_out, left_out, right_out,
    gain_ref, left_ref, x_v, rt, bt, scaled_v, bnd, acc1, acc2, wide, terms, terms_in, grams, ortho_v,
    sib_out, sib_in, cross_out, cross_in, shift_v,
    local_sem, r_recv, r_cross, r_sib, r_fwd, b_recv, b_cross, b_sib, b_fwd,
    t_send, t_recv, g_send, g_recv, o_send, o_recv,
    s_send, s_recv, c_send, c_recv, f_send, f_recv,
):
    me = lax.axis_index("dp")
    section = lax.axis_index("section")
    chips = n // 2
    chip, core = me // 2, me % 2
    sib = chip * 2 + (1 - core)
    tokens, d = x_v.shape
    w = d // n
    pw = w // IN_PIECES
    ow = w // OUT_PIECES

    loads = [
        pltpu.make_async_copy(r_hbm, rt.at[me], local_sem.at[0]),
        pltpu.make_async_copy(x_hbm, x_v, local_sem.at[1]),
        pltpu.make_async_copy(b_hbm, bt.at[me], local_sem.at[2]),
        pltpu.make_async_copy(gain_hbm, gain_ref, local_sem.at[3]),
        pltpu.make_async_copy(left_hbm, left_ref, local_sem.at[4]),
    ]
    for load in loads:
        load.start()

    barrier = pltpu.get_barrier_semaphore()
    for i in range(1, n):
        pl.semaphore_signal(barrier, inc=1, device_id={"dp": (me + i) % n}, device_id_type=pl.DeviceIdType.MESH)

    @pl.when(section < sections - 1)
    def _():
        pl.semaphore_signal(barrier, inc=1, device_id={"section": section + 1}, device_id_type=pl.DeviceIdType.MESH)

    pl.semaphore_wait(barrier, jnp.where(section > 0, n, n - 1))

    def piece(p):
        return pl.ds(pl.multiple_of(p * pw, LANES), pw)

    def columns(j, p):
        return pl.ds(pl.multiple_of(j * w + p * pw, LANES), pw)

    def other(o):
        return ((chip + o) % chips) * 2 + core

    def source(o):
        return ((chip + chips - o) % chips) * 2 + core

    def flip(j):
        return j + 1 - 2 * core

    def to_cross(src, buf, recv, send, o, p):
        return remote(src.at[:, piece(p)], buf.at[me, :, piece(p)], send.at[o, p], recv.at[me, p], dp=other(o))

    def to_sib(src, buf, recv, send, p):
        return remote(src.at[:, piece(p)], buf.at[me, :, piece(p)], send.at[p], recv.at[me, p], dp=sib)

    def forward(buf, recv, send, o, p):
        j = source(o)
        return remote(buf.at[j, :, piece(p)], buf.at[j, :, piece(p)], send.at[o, p], recv.at[j, p], dp=sib)

    def arrived(buf, recv, send, j, p):
        remote(buf.at[j, :, piece(p)], buf.at[j, :, piece(p)], send.at[0], recv.at[j, p], dp=sib).wait_recv()

    for p in range(IN_PIECES):
        for o in range(1, chips):
            to_cross(r_hbm, rt, r_recv, r_cross, o, p).start()
    for p in range(IN_PIECES):
        to_sib(r_hbm, rt, r_recv, r_sib, p).start()
    for p in range(IN_PIECES):
        for o in range(1, chips):
            to_cross(b_hbm, bt, b_recv, b_cross, o, p).start()

    step = d // 12
    loads[1].wait()

    def tiles(i):
        for c in range(step // LANES):
            yield x_v[:, pl.ds(pl.multiple_of(i * step + c * LANES, LANES), LANES)].astype(F32)

    def sum_step(i, acc):
        for tile in tiles(i):
            acc = acc + tile
        return acc

    zero = jnp.zeros((tokens, LANES), F32)
    mu = jnp.sum(lax.fori_loop(0, 12, sum_step, zero), axis=1, keepdims=True) / d
    mu_wide = jnp.broadcast_to(mu, (tokens, LANES))

    def square_step(i, acc):
        for tile in tiles(i):
            c = tile - mu_wide
            acc = acc + c * c
        return acc

    var = jnp.sum(lax.fori_loop(0, 12, square_step, zero), axis=1, keepdims=True) / d
    inverse = lax.rsqrt(var + 1e-5)

    loads[4].wait()
    left = left_ref[...].astype(F32).T.astype(BF16)
    acc1[...] = zero
    acc2[...] = zero
    wide[0] = mu_wide
    wide[1] = jnp.broadcast_to(inverse, (tokens, LANES))

    def first_pass(j, p):
        for c in range(pw // TILE):
            inside = pl.ds(pl.multiple_of(p * pw + c * TILE, LANES), TILE)
            rebuilt_tile = lax.dot_general(left, rt[j, :, inside], NN, preferred_element_type=F32)
            for l in range(TILE // LANES):
                offset = p * pw + c * TILE + l * LANES
                local = pl.ds(pl.multiple_of(offset, LANES), LANES)
                at = pl.ds(pl.multiple_of(j * w + offset, LANES), LANES)
                gain = jnp.broadcast_to(gain_ref[:, at], (8, LANES))[None]
                gain_sum = jnp.zeros((8, LANES), F32)
                bias_sum = jnp.zeros((8, LANES), F32)
                for h in range(0, tokens, ROWS):
                    rows = pl.ds(h, ROWS)
                    shape = (ROWS // 8, 8, LANES)
                    rebuilt = rebuilt_tile[h:h + ROWS, l * LANES:(l + 1) * LANES]
                    normed = (x_v[rows, at].astype(F32) - wide[0, rows, :]) * wide[1, rows, :]
                    product = (rebuilt * normed).reshape(shape)
                    rebuilt = rebuilt.reshape(shape)
                    gain_sum = gain_sum + jnp.sum(product, axis=0)
                    bias_sum = bias_sum + jnp.sum(rebuilt, axis=0)
                    scaled = (rebuilt * gain).reshape(ROWS, LANES)
                    scaled_v[rows, at] = scaled
                    acc1[rows, :] += scaled
                    acc2[rows, :] += (product * gain).reshape(ROWS, LANES)
                terms[j, 0:1, local] = jnp.sum(gain_sum, axis=0, keepdims=True)
                terms[j, 1:2, local] = jnp.sum(bias_sum, axis=0, keepdims=True)

    def loop(count, body):
        lax.fori_loop(0, count, lambda i, _: (body(i), 0)[1], 0)

    loads[0].wait()
    loads[3].wait()
    loop(IN_PIECES, lambda p: first_pass(me, p))

    def sib_first(p):
        arrived(rt, r_recv, r_sib, sib, p)
        first_pass(sib, p)

    loop(IN_PIECES, sib_first)

    def cross_first(i):
        p, o = i // (chips - 1), 1 + i % (chips - 1)
        arrived(rt, r_recv, r_sib, source(o), p)
        forward(rt, r_recv, r_fwd, o, p).start()
        first_pass(source(o), p)

    loop(IN_PIECES * (chips - 1), cross_first)
    loop(IN_PIECES, lambda p: to_sib(b_hbm, bt, b_recv, b_sib, p).start())

    def forwarded_first(i):
        p, o = i // (chips - 1), 1 + i % (chips - 1)
        arrived(rt, r_recv, r_sib, flip(source(o)), p)
        first_pass(flip(source(o)), p)

    loop(IN_PIECES * (chips - 1), forwarded_first)

    m1 = jnp.sum(acc1[...], axis=1, keepdims=True) / d * inverse
    m2 = jnp.sum(acc2[...], axis=1, keepdims=True) / d * inverse * inverse

    wide[0] = jnp.broadcast_to(m1 - mu * m2, (tokens, LANES))
    wide[2] = jnp.broadcast_to(m2, (tokens, LANES))

    def second_pass(j, p):
        for h in range(0, tokens, ROWS):
            rows = pl.ds(h, ROWS)
            shift, scale, slope = wide[0, rows, :], wide[1, rows, :], wide[2, rows, :]
            for l in range(pw // LANES):
                at = pl.ds(pl.multiple_of(j * w + p * pw + l * LANES, LANES), LANES)
                bnd[rows, at] = (scaled_v[rows, at] * scale - x_v[rows, at].astype(F32) * slope - shift).astype(BF16)

    def project(j, p):
        acc1[0:64, :] += lax.dot_general(bt[j, :, piece(p)], bnd[:, columns(j, p)], NT, preferred_element_type=F32)

    acc1[...] = zero
    loads[2].wait()

    def own_second(p):
        second_pass(me, p)
        project(me, p)

    loop(IN_PIECES, own_second)

    def sib_second(p):
        second_pass(sib, p)
        arrived(bt, b_recv, b_sib, sib, p)
        project(sib, p)

    loop(IN_PIECES, sib_second)

    def cross_second(i):
        p, o = i // (chips - 1), 1 + i % (chips - 1)
        second_pass(source(o), p)
        second_pass(flip(source(o)), p)
        arrived(bt, b_recv, b_sib, source(o), p)
        forward(bt, b_recv, b_fwd, o, p).start()
        project(source(o), p)

    loop(IN_PIECES * (chips - 1), cross_second)

    def forwarded_second(i):
        p, o = i // (chips - 1), 1 + i % (chips - 1)
        arrived(bt, b_recv, b_sib, flip(source(o)), p)
        project(flip(source(o)), p)

    loop(IN_PIECES * (chips - 1), forwarded_second)

    r = left_ref.shape[0]
    power = acc1[0:64, :]
    half = r // 2
    tall = jnp.concatenate([power, jnp.zeros_like(power)], axis=0)
    low = jnp.concatenate([jnp.zeros_like(power), power], axis=0)
    grams[me] = lax.dot_general(
        power[0:half], tall, NT, precision=HIGH, preferred_element_type=F32
    ) + lax.dot_general(power[half:r], low, NT, precision=HIGH, preferred_element_type=F32)

    def gram_copy(i):
        return remote(grams.at[me], grams.at[me], g_send.at[i], g_recv.at[me], dp=(me + i) % n)

    def terms_copy(i):
        to = (me + i) % n
        return remote(terms.at[to], terms_in.at[me], t_send.at[i], t_recv.at[me], dp=to)

    for i in range(1, n):
        gram_copy(i).start()
    for i in range(1, n):
        j = (me + i) % n
        remote(grams.at[j], grams.at[j], g_send.at[0], g_recv.at[j], dp=sib).wait_recv()
    for i in range(1, n):
        terms_copy(i).start()
    packed = grams[0]
    for j in range(1, n):
        packed = packed + grams[j]
    factor = inverse_factor(jnp.concatenate([packed, pltpu.roll(packed, r, 1)], axis=0))
    ortho = lax.dot_general(factor, low, NN, precision=HIGH, preferred_element_type=F32).astype(BF16)
    ortho_v[...] = ortho

    def ortho_copy():
        return remote(ortho_v, left_out, o_send, o_recv, section=section - 1)

    @pl.when(section > 0)
    def _():
        ortho_copy().start()

    def out_piece(q):
        return pl.ds(pl.multiple_of(q * ow, LANES), ow)

    def share(j, q):
        at = pl.ds(pl.multiple_of(j * w + q * ow, LANES), ow)
        return lax.dot_general(ortho_v[...], bnd[:, at], NN, preferred_element_type=F32)

    def sib_copy(o, q):
        return remote(sib_out.at[o, :, out_piece(q)], sib_in.at[o, :, out_piece(q)], s_send.at[o, q], s_recv.at[o, q], dp=sib)

    def cross_copy(o, q):
        return remote(cross_out.at[o, :, out_piece(q)], cross_in.at[o, :, out_piece(q)], c_send.at[o, q], c_recv.at[o, q], dp=other(o))

    def shift_copy(q):
        return remote(shift_v.at[:, out_piece(q)], right_out.at[:, out_piece(q)], f_send.at[q], f_recv.at[q], section=section - 1)

    def send_sib(o, q):
        sib_out[o, :, out_piece(q)] = share(flip(other(o)), q).astype(BF16)
        sib_copy(o, q).start()

    def split(i):
        return 1 + i % (chips - 1), i // (chips - 1)

    def stage_a(i):
        o, q = split(i)
        send_sib(o, q)

    loop(OUT_PIECES * (chips - 1), stage_a)

    def stage_b(i):
        o, q = split(i)
        mine = share(other(o), q)
        sib_copy(o, q).wait_recv()
        cross_out[o, :, out_piece(q)] = (mine + sib_in[o, :, out_piece(q)].astype(F32)).astype(BF16)
        cross_copy(o, q).start()

    loop(OUT_PIECES * (chips - 1), stage_b)
    loop(OUT_PIECES, lambda q: send_sib(0, q))

    for i in range(1, n):
        j = (me + i) % n
        remote(terms.at[j], terms_in.at[j], t_send.at[0], t_recv.at[j], dp=sib).wait_recv()
    sums = terms[me]
    for i in range(1, n):
        sums = sums + terms_in[(me + i) % n]
    sums = sums * (1.0 / tokens_all ** 0.5)
    gain_out[...] = sums[0:1]
    bias_out[...] = sums[1:2]

    def stage_c(q):
        total = share(me, q)
        sib_copy(0, q).wait_recv()
        total = total + sib_in[0, :, out_piece(q)].astype(F32)
        for o in range(1, chips):
            cross_copy(o, q).wait_recv()
            total = total + cross_in[o, :, out_piece(q)].astype(F32)
        shift_v[:, out_piece(q)] = total.astype(BF16)

        @pl.when(section > 0)
        def _():
            shift_copy(q).start()

    loop(OUT_PIECES, stage_c)

    @pl.when(section == sections - 1)
    def _():
        left_out[...] = jnp.zeros_like(left_out)
        right_out[...] = jnp.zeros_like(right_out)

    def inputs_sent(i):
        p, o = i // (chips - 1), 1 + i % (chips - 1)
        to_cross(r_hbm, rt, r_recv, r_cross, o, p).wait_send()
        to_cross(b_hbm, bt, b_recv, b_cross, o, p).wait_send()
        forward(rt, r_recv, r_fwd, o, p).wait_send()
        forward(bt, b_recv, b_fwd, o, p).wait_send()

    loop(IN_PIECES * (chips - 1), inputs_sent)

    def inputs_sent_sib(p):
        to_sib(r_hbm, rt, r_recv, r_sib, p).wait_send()
        to_sib(b_hbm, bt, b_recv, b_sib, p).wait_send()

    loop(IN_PIECES, inputs_sent_sib)
    for i in range(1, n):
        gram_copy(i).wait_send()
        terms_copy(i).wait_send()

    def shares_sent(i):
        o, q = split(i)
        sib_copy(o, q).wait_send()
        cross_copy(o, q).wait_send()

    loop(OUT_PIECES * (chips - 1), shares_sent)
    loop(OUT_PIECES, lambda q: sib_copy(0, q).wait_send())

    @pl.when(section < sections - 1)
    def _():
        ortho_copy().wait_recv()
        loop(OUT_PIECES, lambda q: shift_copy(q).wait_recv())

    @pl.when(section > 0)
    def _():
        ortho_copy().wait_send()
        loop(OUT_PIECES, lambda q: shift_copy(q).wait_send())


def write_out(*refs):
    come = [pltpu.make_async_copy(refs[i], refs[8 + i], refs[12].at[i]) for i in range(4)]
    go = [pltpu.make_async_copy(refs[8 + i], refs[4 + i], refs[13].at[i]) for i in range(4)]
    for copy in come:
        copy.start()
    for first, second in zip(come, go):
        first.wait()
        second.start()
    for copy in go:
        copy.wait()


def on_device(n, sections, saved_input, norm_gain, left_in, right_in, basis):
    _, tokens, d = saved_input.shape
    r = left_in.shape[2]
    w = d // n
    chips = n // 2
    vmem = pl.BlockSpec(memory_space=pltpu.VMEM)
    hbm = pl.BlockSpec(memory_space=pltpu.HBM)
    dma = pltpu.SemaphoreType.DMA
    gather = [dma((n, IN_PIECES)), dma((chips, IN_PIECES)), dma((IN_PIECES,)), dma((chips, IN_PIECES))]
    results = (
        jax.ShapeDtypeStruct((1, w), F32),
        jax.ShapeDtypeStruct((1, w), F32),
        jax.ShapeDtypeStruct((r, tokens), BF16),
        jax.ShapeDtypeStruct((r, w), BF16),
    )
    held = pl.pallas_call(
        functools.partial(kernel, n, sections, tokens * n),
        out_shape=results,
        in_specs=[hbm] * 5,
        out_specs=(vmem, vmem, vmem, vmem),
        scratch_shapes=[
            pltpu.VMEM((1, d), F32),
            pltpu.VMEM((r, tokens), BF16),
            pltpu.VMEM((tokens, d), BF16),
            pltpu.VMEM((n, r, w), BF16),
            pltpu.VMEM((n, r, w), BF16),
            pltpu.VMEM((tokens, d), F32),
            pltpu.VMEM((tokens, d), BF16),
            pltpu.VMEM((tokens, LANES), F32),
            pltpu.VMEM((tokens, LANES), F32),
            pltpu.VMEM((3, tokens, LANES), F32),
            pltpu.VMEM((n, 2, w), F32),
            pltpu.VMEM((n, 2, w), F32),
            pltpu.VMEM((n, r // 2, 2 * r), F32),
            pltpu.VMEM((r, tokens), BF16),
            pltpu.VMEM((chips, r, w), BF16),
            pltpu.VMEM((chips, r, w), BF16),
            pltpu.VMEM((chips, r, w), BF16),
            pltpu.VMEM((chips, r, w), BF16),
            pltpu.VMEM((r, w), BF16),
            dma((5,)),
            *gather,
            *gather,
            dma((n,)), dma((n,)),
            dma((n,)), dma((n,)),
            dma, dma,
            dma((chips, OUT_PIECES)), dma((chips, OUT_PIECES)),
            dma((chips, OUT_PIECES)), dma((chips, OUT_PIECES)),
            dma((OUT_PIECES,)), dma((OUT_PIECES,)),
        ],
        compiler_params=pltpu.CompilerParams(
            collective_id=0, has_side_effects=True, vmem_limit_bytes=63 * 1024 * 1024
        ),
    )(saved_input[0], norm_gain, left_in[0].T, right_in[0].T, basis[0].T)
    gain, bias, left, right = pl.pallas_call(
        write_out,
        out_shape=results,
        in_specs=[hbm] * 4,
        out_specs=(hbm,) * 4,
        scratch_shapes=[*(pltpu.VMEM(a.shape, a.dtype) for a in results), dma((4,)), dma((4,))],
        compiler_params=pltpu.CompilerParams(vmem_limit_bytes=63 * 1024 * 1024),
    )(*held)
    return gain, bias, left.T[None], right.T[None]


def solution(mesh):
    placed = (
        P("section", "dp", None),
        P("section", None),
        P("section", "dp", None),
        P("section", "dp", None),
        P("section", "dp", None),
    )
    return jax.shard_map(
        functools.partial(on_device, mesh.shape["dp"], mesh.shape["section"]),
        mesh=mesh,
        in_specs=placed,
        out_specs=(
            P("section", "dp"),
            P("section", "dp"),
            P("section", "dp", None),
            P("section", "dp", None),
        ),
        check_vma=False,
    )
```
